256 devices in a mesh: row: 8 (over y, core), col: 32 (over x, z).
Axes of the slice: x: 4, y: 4, z: 8, core: 2. Of those that a mesh axis runs over, the one named last changes fastest.
Arguments:
- observed: float32 [16, 64, 4096], P(None, 'row', 'col'), may hold values from -6 to 6
- coef_maps: float32 [96, 64, 4096], P(None, 'row', 'col'), may hold values from -1.2 to 1.2
- dictionary: float32 [96, 784], replicated, may hold values from -9 to 9
- consensus: float32 [96, 784], replicated, may hold values from -4 to 4
- dual_vars: float32 [96, 784], replicated, may hold values from -1.8 to 1.8
Outputs:
- new_maps: float32 [96, 64, 4096], P(None, 'row', 'col')
- new_dictionary: float32 [96, 784], replicated
- new_consensus: float32 [96, 784], replicated
- new_duals: float32 [96, 784], replicated
The draws below stay inside these ranges and needn't reach their ends.
All inputs are finite; a program needn't handle non-finite values.
Results may differ from the reference program's by a relative error of at most 0.0003.
Values sent between devices are 32-bit elements; how exact they have to be, the bound alone decides.
No kernel may reach another device: no remote copies, remote signals or barrier semaphores. Data moves between devices by JAX's collectives and lax.ppermute only.
A program may use at most 128 MiB of HBM per device.

```python
import math
import jax
import jax.numpy as jnp
from jax import lax

M = 96
C = 16
K = 7
ITERS = 2
NH = 64
NW = 4096


def draw_dictionary(key, part):
    scale_key = jax.random.fold_in(key, 11)
    entry_key = jax.random.fold_in(key, 12)
    logs = jax.random.uniform(scale_key, (M, 1), jnp.float32, jnp.log(0.7), jnp.log(2.2))
    scales = jnp.exp(logs)
    entries = jnp.clip(jax.random.normal(entry_key, (M, C * K * K), jnp.float32), -4.0, 4.0)
    return (entries * scales).astype(jnp.float32)


def levels(own_key, shape, split, low, largest):
    factor_of = 1.0
    for dim, shards_of in split:
        steps = jax.random.uniform(jax.random.fold_in(jax.random.fold_in(own_key, 6), dim), (shards_of,), jnp.float32, low / len(split), largest / len(split))
        factor_of = factor_of * jnp.repeat(jnp.exp(steps), shape[dim] // shards_of).reshape((-1,) + (1,) * (len(shape) - 1 - dim))
    return factor_of


def gaussian(rng, extent, scale, most, cuts=(), kind=jnp.bfloat16):
    array = jax.random.normal(rng, extent, jnp.float32) * scale
    if len(cuts) > 0:
        array = levels(rng, extent, cuts, -0.22, 0.18) * array
    return jnp.clip(array, min=-most, max=most).astype(kind)


def setup_inputs(seed: int = 0) -> dict:
    key_of = jax.random.split(jax.random.key(seed), 6)
    return {
        "observed": gaussian(key_of[0], (C, NH, NW), 1.0, 6.0, ((1, 8), (2, 32)), jnp.float32),
        "coef_maps": gaussian(key_of[1], (M, NH, NW), 0.2, 1.2, ((1, 8), (2, 32)), jnp.float32),
        "dictionary": draw_dictionary(jax.random.fold_in(key_of[5], 71), 0),
        "consensus": gaussian(key_of[3], (M, C * K * K), 1.0, 4.0, (), jnp.float32),
        "dual_vars": gaussian(key_of[4], (M, C * K * K), 0.3, 1.8, (), jnp.float32),
    }


step_coef = 0.5
sparsity = 0.1
dict_step = 0.08
penalty = 2.0
HIGH = lax.Precision.HIGHEST

def recon_taps(padded, filters, out_rows, out_cols):

    def advance(index, summed):
        index = index.astype(jnp.int32)
        row_tap = index // K
        col_tap = index % K
        zero = jnp.int32(0)
        window = lax.dynamic_slice(padded, (zero, row_tap, col_tap), (M, out_rows, out_cols))
        weights = lax.dynamic_slice(filters, (zero, zero, row_tap, col_tap), (M, C, 1, 1)).reshape(M, C)
        return summed + jnp.einsum('mc,mhw->chw', weights, window, precision=HIGH)
    start = jnp.zeros((C, out_rows, out_cols), padded.dtype)
    return lax.fori_loop(0, K * K, advance, start)

def corr_taps(padded, filters, out_rows, out_cols):
    reach = K // 2

    def advance(index, summed):
        index = index.astype(jnp.int32)
        row_tap = index // K
        col_tap = index % K
        zero = jnp.int32(0)
        window = lax.dynamic_slice(padded, (zero, 2 * reach - row_tap, 2 * reach - col_tap), (C, out_rows, out_cols))
        weights = lax.dynamic_slice(filters, (zero, zero, row_tap, col_tap), (M, C, 1, 1)).reshape(M, C)
        return summed + jnp.einsum('mc,chw->mhw', weights, window, precision=HIGH)
    start = jnp.zeros((M, out_rows, out_cols), padded.dtype)
    return lax.fori_loop(0, K * K, advance, start)

def grad_taps(padded, resid, out_rows, out_cols):

    def one_tap(index):
        index = index.astype(jnp.int32)
        row_tap = index // K
        col_tap = index % K
        zero = jnp.int32(0)
        window = lax.dynamic_slice(padded, (zero, row_tap, col_tap), (M, out_rows, out_cols))
        return jnp.einsum('mhw,chw->mc', window, resid, precision=HIGH)
    stacked = lax.map(one_tap, jnp.arange(K * K, dtype=jnp.int32))
    return jnp.transpose(stacked, (1, 2, 0)).reshape(M, C * K * K)

def reference(observed, coef_maps, dictionary, consensus, dual_vars):
    reach = K // 2
    norm_scale = 1.0 / math.sqrt(M * K * K)
    maps_now = coef_maps
    filt_now = dictionary
    cons_now = consensus
    duals_now = dual_vars
    height = observed.shape[1]
    width = observed.shape[2]
    for sweep in range(ITERS):
        filters = filt_now.reshape(M, C, K, K)
        padded = jnp.pad(maps_now, ((0, 0), (reach, reach), (reach, reach)))
        recon = norm_scale * recon_taps(padded, filters, height, width)
        resid = recon - observed
        resid_pad = jnp.pad(resid, ((0, 0), (reach, reach), (reach, reach)))
        corr = norm_scale * corr_taps(resid_pad, filters, height, width)
        grad = norm_scale * grad_taps(padded, resid, height, width)
        moved = maps_now - step_coef * corr
        limit = step_coef * sparsity
        maps_now = moved - jnp.clip(moved, -limit, limit)
        filt_now = filt_now - dict_step * (grad + penalty * (filt_now - cons_now + duals_now))
        joined = filt_now + duals_now
        spread = jnp.sqrt(lax.optimization_barrier(jnp.mean(joined * joined, axis=1, keepdims=True)))
        cons_now = joined / jnp.maximum(1.0, spread)
        duals_now = duals_now + filt_now - cons_now
    return (maps_now, filt_now, cons_now, duals_now)
```

```python
import functools
import math

import jax
import jax.numpy as jnp
from jax import lax
from jax.experimental import pallas as pl
from jax.experimental.pallas import tpu as pltpu
from jax.sharding import PartitionSpec as P

M = 96
C = 16
K = 7
REACH = 3
ITERS = 2
ROWS = 8
LANES = 128
PAD_ROWS = ROWS + 2 * REACH
TAPS = K * K
FLAT = C * TAPS
WIDE = K * LANES
D_ROWS = K * M
G_ROWS = 704
SLAB = 8 * M

step_coef = 0.5
sparsity = 0.1
dict_step = 0.08
penalty = 2.0
norm_scale = 1.0 / math.sqrt(M * K * K)

F32 = jnp.float32
BF16 = jnp.bfloat16


def shape(*dims):
    return jax.ShapeDtypeStruct(dims, F32)


def call(kernel, outs, scratch=()):
    return pl.pallas_call(
        kernel,
        out_shape=outs,
        scratch_shapes=list(scratch),
        compiler_params=pltpu.CompilerParams(vmem_limit_bytes=28 * 1024 * 1024),
    )


def split2(value):
    high = value.astype(BF16)
    return high, (value - high.astype(F32)).astype(BF16)


def split3(value):
    high = value.astype(BF16)
    rest = value - high.astype(F32)
    mid = rest.astype(BF16)
    return high, mid, (rest - mid.astype(F32)).astype(BF16)


def roll(value, shift):
    shift = shift % LANES
    return value if shift == 0 else pltpu.roll(value, shift, 1)


def lane_of(rows):
    return lax.broadcasted_iota(jnp.int32, (rows, LANES), 1)


def matmul(a, b):
    return jnp.dot(a, b, preferred_element_type=F32)


def matmul_nt(a, b):
    return lax.dot_general(a, b, (((1,), (1,)), ((), ())), preferred_element_type=F32)


def rows_kernel(maps, by_row, top, bottom):
    for y in range(ROWS):
        value = maps[:, y, :]
        by_row[y * M : (y + 1) * M, :] = value
        if y < REACH:
            top[y * M : (y + 1) * M, :] = value
        if y >= ROWS - REACH:
            at = (y - ROWS + REACH) * M
            bottom[at : at + M, :] = value


def flat_of(lane):
    row_tap = lane >> 7
    col_tap = (lane >> 4) & 7
    band = lane & 15
    return jnp.where(col_tap < K, band * TAPS + row_tap * K + col_tap, -1)


def to_rows_kernel(filt, cons, duals, filt_out, cons_out, duals_out, stacked):
    stacked[:, 6 * LANES :] = jnp.zeros((9 * M, LANES), BF16)
    for i, ref in enumerate((filt, cons, duals)):
        for j, part in enumerate(split3(ref[...])):
            at = (3 * i + j) * M
            stacked[at : at + M, :FLAT] = part
    source = lax.broadcasted_iota(jnp.int32, (WIDE, LANES), 0)
    lane = lane_of(WIDE)
    for a in range(K):
        pick = (source == flat_of(lane + a * LANES)).astype(F32).astype(BF16)
        moved = matmul(stacked[...], pick)
        for i, ref in enumerate((filt_out, cons_out, duals_out)):
            at = 3 * i * M
            ref[a * M : (a + 1) * M, :] = (
                moved[at : at + M] + moved[at + M : at + 2 * M] + moved[at + 2 * M : at + 3 * M]
            )


def padded_row(y, size, own, above, below):
    if y < REACH:
        return above[y * size : (y + 1) * size, :]
    if y < REACH + ROWS:
        at = (y - REACH) * size
        return own[at : at + size, :]
    at = (y - REACH - ROWS) * size
    return below[at : at + size, :]


def pack_kernel(size, own, above, below, left_edge, right_edge):
    lane = lane_of(size)
    left = jnp.zeros((size, LANES), F32)
    right = jnp.zeros((size, LANES), F32)
    for y in range(PAD_ROWS):
        value = padded_row(y, size, own, above, below)
        here = (lane >= 3 * y) & (lane < 3 * y + 3)
        left = jnp.where(here, roll(value, 3 * y), left)
        right = jnp.where(here, roll(value, 3 * y + 3), right)
    left_edge[...] = left
    right_edge[...] = right


def neighbours(axis, toward_high, toward_low):
    count = lax.axis_size(axis)
    up = [(i, i + 1) for i in range(count - 1)]
    down = [(i + 1, i) for i in range(count - 1)]
    return lax.ppermute(toward_high, axis, up), lax.ppermute(toward_low, axis, down)


def halos(size, own, top, bottom):
    above, below = neighbours("row", bottom, top)
    left_edge, right_edge = call(
        functools.partial(pack_kernel, size), [shape(size, LANES)] * 2
    )(own, above, below)
    left, right = neighbours("col", right_edge, left_edge)
    return above, below, left, right


def recon_and_grad(
    maps, above, below, left, right, observed, filt,
    resid_out, top, bottom, grad, x_hi, x_lo, h_hi, h_lo, r_all, r_edge,
):
    for y in range(PAD_ROWS):
        hi, lo = split2(padded_row(y, M, maps, above, below))
        for ref, part in ((x_hi, hi), (x_lo, lo)):
            ref[y * M : (y + 1) * M, :LANES] = part
            if y > 0:
                ref[(y - 1) * M : y * M, LANES:] = part
    for ref in (x_hi, x_lo):
        ref[(PAD_ROWS - 1) * M :, LANES:] = jnp.zeros((M, LANES), BF16)
    edge = jnp.where(lane_of(M) < 64, right[...], roll(left[...], 64))
    for a in range(K):
        hi, lo = split2(roll(edge, -3 * a))
        h_hi[a * M : (a + 1) * M, :] = hi
        h_lo[a * M : (a + 1) * M, :] = lo
    for ref in (h_hi, h_lo):
        ref[D_ROWS:, :] = jnp.zeros((SLAB - D_ROWS, LANES), BF16)

    turned = jnp.concatenate([filt, jnp.zeros((SLAB - D_ROWS, LANES), F32)], axis=0).T
    d_hi, d_lo = split2(turned)
    d_both = jnp.concatenate([d_hi, d_lo], axis=0)

    def apply(hi, lo):
        both = matmul(d_both, hi)
        return both[:LANES] + both[LANES:] + matmul(d_hi, lo)

    lane = lane_of(C)
    at_edge = apply(h_hi[...], h_lo[...])
    resid = []
    for y in range(0, ROWS, 2):
        planes = apply(x_hi[y * M : y * M + SLAB, :], x_lo[y * M : y * M + SLAB, :])
        for k in range(2):
            row = y + k
            total = jnp.zeros((C, LANES), F32)
            for b in range(K):
                d = b - REACH
                own = roll(planes[b * C : (b + 1) * C, k * LANES : (k + 1) * LANES], -d)
                band_edge = at_edge[b * C : (b + 1) * C, :]
                if d > 0:
                    moved = roll(band_edge, 131 - b - 3 * row)
                    own = jnp.where(lane >= LANES - d, moved, own)
                elif d < 0:
                    moved = roll(band_edge, -(64 + 3 * row) - b)
                    own = jnp.where(lane < -d, moved, own)
                total = total + own
            value = norm_scale * total - observed[:, row, :]
            resid.append(value)
            resid_out[row * C : (row + 1) * C, :] = value
            if row < REACH:
                top[row * C : (row + 1) * C, :] = value
            if row >= ROWS - REACH:
                at = (row - ROWS + REACH) * C
                bottom[at : at + C, :] = value

    zero16 = jnp.zeros((C, LANES), F32)
    for b in range(K):
        d = b - REACH
        near = zero16
        for row in range(ROWS):
            moved = roll(resid[row], d)
            if d > 0:
                moved = jnp.where(lane >= d, moved, 0.0)
                here = (lane >= 3 * row) & (lane < 3 * row + d)
                near = jnp.where(here, roll(resid[row], 3 * row - 131 + b), near)
            elif d < 0:
                moved = jnp.where(lane < LANES + d, moved, 0.0)
                here = (lane >= 64 + 3 * row + b) & (lane < 64 + 3 * row + 3)
                near = jnp.where(here, roll(resid[row], 64 + 3 * row + b), near)
            hi, lo = split2(moved)
            r_all[b * C : (b + 1) * C, row * LANES : (row + 1) * LANES] = hi
            r_all[LANES + b * C : LANES + (b + 1) * C, row * LANES : (row + 1) * LANES] = lo
        hi, lo = split2(near)
        r_edge[b * C : (b + 1) * C, :] = hi
        r_edge[LANES + b * C : LANES + (b + 1) * C, :] = lo
    for at in (K * C, LANES + K * C):
        r_all[at : at + C, :] = jnp.zeros((C, ROWS * LANES), BF16)
        r_edge[at : at + C, :] = jnp.zeros((C, LANES), BF16)

    def gather(hi, lo, spread):
        both = matmul_nt(hi, spread)
        return both[:, :LANES] + both[:, LANES:] + matmul_nt(lo, spread[:LANES])

    total = gather(h_hi[:D_ROWS, :], h_lo[:D_ROWS, :], r_edge[...])
    for y in range(0, ROWS, 2):
        total = total + gather(
            x_hi[y * M : y * M + D_ROWS, :],
            x_lo[y * M : y * M + D_ROWS, :],
            r_all[:, y * LANES : (y + 2) * LANES],
        )
    grad[:D_ROWS, :] = total
    grad[D_ROWS:, :] = jnp.zeros((G_ROWS - D_ROWS, LANES), F32)


RECON_OUT = [shape(ROWS * C, LANES), shape(3 * C, LANES), shape(3 * C, LANES), shape(G_ROWS, LANES)]
RECON_SCRATCH = [
    pltpu.VMEM((PAD_ROWS * M, 2 * LANES), BF16),
    pltpu.VMEM((PAD_ROWS * M, 2 * LANES), BF16),
    pltpu.VMEM((SLAB, LANES), BF16),
    pltpu.VMEM((SLAB, LANES), BF16),
    pltpu.VMEM((2 * LANES, ROWS * LANES), BF16),
    pltpu.VMEM((2 * LANES, LANES), BF16),
]


def updated(summed, filt, cons, duals, keep):
    squares = jnp.zeros((M, LANES), F32)
    for a in range(K):
        at = slice(a * M, (a + 1) * M)
        now, dual = filt[at, :], duals[at, :]
        after = now - dict_step * (norm_scale * summed[at, :] + penalty * (now - cons[at, :] + dual))
        joined = after + dual
        squares = squares + joined * joined
        keep(0, a, after)
        keep(1, a, joined)
    spread = jnp.sqrt(jnp.sum(squares, axis=1, keepdims=True) / FLAT)
    return 1.0 / jnp.maximum(1.0, spread)


def first_kernel(maps, above, below, left, right, observed, filt, *rest):
    recon_and_grad(maps, above, below, left, right, observed, filt[...], *rest)


def next_kernel(
    summed, filt, cons, duals, maps, above, below, left, right, observed,
    filt_out, cons_out, duals_out, *rest,
):
    update_into(summed, filt, cons, duals, filt_out, cons_out, duals_out)
    recon_and_grad(maps, above, below, left, right, observed, filt_out[...], *rest)


def update_into(summed, filt, cons, duals, filt_out, cons_out, duals_out):
    refs = (filt_out, cons_out)

    def keep(which, a, value):
        refs[which][a * M : (a + 1) * M, :] = value

    factor = updated(summed, filt, cons, duals, keep)
    for a in range(K):
        at = slice(a * M, (a + 1) * M)
        joined = cons_out[at, :]
        projected = joined * factor
        cons_out[at, :] = projected
        duals_out[at, :] = joined - projected


def last_kernel(summed, filt, cons, duals, filt_out, cons_out, duals_out, new, stacked):
    update_into(summed, filt, cons, duals, new.at[0], new.at[1], new.at[2])
    for i in range(3):
        for a in range(K):
            for j, part in enumerate(split3(new[i, a * M : (a + 1) * M, :])):
                at = (3 * i + j) * M
                stacked[at : at + M, a * LANES : (a + 1) * LANES] = part
    source = lax.broadcasted_iota(jnp.int32, (WIDE, LANES), 0)
    wanted = flat_of(source)
    for block in range(K):
        target = lane_of(WIDE) + block * LANES
        pick = (wanted == target).astype(F32).astype(BF16)
        moved = matmul(stacked[...], pick)
        width = min(LANES, FLAT - block * LANES)
        for i, ref in enumerate((filt_out, cons_out, duals_out)):
            at = 3 * i * M
            value = moved[at : at + M] + moved[at + M : at + 2 * M] + moved[at + 2 * M : at + 3 * M]
            ref[:, block * LANES : block * LANES + width] = value[:, :width]


def corr_kernel(last, resid, above, below, left, right, filt, maps, *rest):
    if last:
        maps_out, s_hi, s_lo = rest
    else:
        maps_out, top, bottom, s_hi, s_lo = rest
    lane = lane_of(C)
    for y in range(PAD_ROWS - 1 + 1):
        own = padded_row(y, C, resid, above, below)
        edge = jnp.where(lane < 3, roll(right[...], -3 * y), roll(left[...], 125 - 3 * y))
        for b in range(K + 1):
            if b < K:
                d = b - REACH
                value = own
                if d > 0:
                    value = jnp.where(lane >= LANES - d, edge, own)
                elif d < 0:
                    value = jnp.where(lane < -d, edge, own)
                hi, lo = split2(roll(value, d))
            else:
                hi = lo = jnp.zeros((C, LANES), BF16)
            for ref, part in ((s_hi, hi), (s_lo, lo)):
                at = y * LANES + b * C
                if y < PAD_ROWS - 1:
                    ref[at : at + C, :LANES] = part
                if y > 0:
                    ref[at - LANES : at - LANES + C, LANES:] = part

    across = jnp.concatenate([filt[(6 - q) * M : (7 - q) * M, :] for q in range(K)], axis=1)
    d_hi, d_lo = split2(across)
    d_both = jnp.concatenate([d_hi, d_lo], axis=0)
    limit = step_coef * sparsity
    for y in range(0, ROWS, 2):
        slab = slice(y * LANES, y * LANES + WIDE)
        both = matmul(d_both, s_hi[slab, :])
        corr = both[:M] + both[M:] + matmul(d_hi, s_lo[slab, :])
        for k in range(2):
            row = y + k
            moved = maps[row * M : (row + 1) * M, :] - (step_coef * norm_scale) * corr[
                :, k * LANES : (k + 1) * LANES
            ]
            value = moved - jnp.clip(moved, -limit, limit)
            if last:
                maps_out[:, row, :] = value
                continue
            maps_out[row * M : (row + 1) * M, :] = value
            if row < REACH:
                top[row * M : (row + 1) * M, :] = value
            if row >= ROWS - REACH:
                at = (row - ROWS + REACH) * M
                bottom[at : at + M, :] = value


CORR_SCRATCH = [pltpu.VMEM(((PAD_ROWS - 1) * LANES, 2 * LANES), BF16)] * 2


def pairs_row(change):
    return [(i, change(i // 2, i % 2)) for i in range(8)]


def pairs_col(change):
    return [(i, change(i // 8, i % 8)) for i in range(32)]


def swap_even(i):
    return i ^ 1


def swap_odd(i, count):
    return (i + 1) % count if i % 2 == 1 else (i - 1) % count


THIRD = {2: 5, 5: 2, 1: 6, 6: 1, 3: 0, 0: 3, 4: 7, 7: 4}
CORE = pairs_row(lambda y, core: y * 2 + 1 - core)
Y_EVEN = pairs_row(lambda y, core: swap_even(y) * 2 + core)
Y_ODD = pairs_row(lambda y, core: swap_odd(y, 4) * 2 + core)
COLS = [
    pairs_col(lambda x, z: swap_even(x) * 8 + z),
    pairs_col(lambda x, z: swap_odd(x, 4) * 8 + z),
    pairs_col(lambda x, z: x * 8 + swap_even(z)),
    pairs_col(lambda x, z: x * 8 + swap_odd(z, 8)),
    pairs_col(lambda x, z: x * 8 + THIRD[z]),
]


def halves(value, bit):
    half = value.shape[0] // 2
    low, high = value[:half], value[half:]
    return jnp.where(bit == 0, high, low), jnp.where(bit == 0, low, high)


def joined(mine, other, bit):
    return jnp.where(
        bit == 0, jnp.concatenate([mine, other]), jnp.concatenate([other, mine])
    )


def sum_all(grad):
    row = lax.axis_index("row")
    y = row // 2
    bits = [(row % 2, CORE), ((y == 1) | (y == 2), Y_EVEN), ((y == 2) | (y == 3), Y_ODD)]
    bits = [(bit.astype(jnp.int32), pairs) for bit, pairs in bits]
    value = grad
    for bit, pairs in bits:
        sent, kept = halves(value, bit)
        value = kept + lax.ppermute(sent, "row", pairs)
    for pairs in COLS:
        value = value + lax.ppermute(value, "col", pairs)
    for bit, pairs in reversed(bits):
        value = joined(value, lax.ppermute(value, "row", pairs), bit)
    return value


def local(observed, coef_maps, dictionary, consensus, dual_vars):
    map_rows = [shape(ROWS * M, LANES), shape(3 * M, LANES), shape(3 * M, LANES)]
    filters = [shape(D_ROWS, LANES)] * 3
    maps, top, bottom = call(rows_kernel, map_rows)(coef_maps)
    filt, cons, duals = call(to_rows_kernel, filters, [pltpu.VMEM((9 * M, WIDE), BF16)])(
        dictionary, consensus, dual_vars
    )
    edges = halos(M, maps, top, bottom)
    resid, r_top, r_bottom, grad = call(first_kernel, RECON_OUT, RECON_SCRATCH)(
        maps, *edges, observed, filt
    )
    summed = sum_all(grad)
    r_edges = halos(C, resid, r_top, r_bottom)
    maps, top, bottom = call(functools.partial(corr_kernel, False), map_rows, CORR_SCRATCH)(
        resid, *r_edges, filt, maps
    )
    edges = halos(M, maps, top, bottom)
    filt, cons, duals, resid, r_top, r_bottom, grad = call(
        next_kernel, filters + RECON_OUT, RECON_SCRATCH
    )(summed, filt, cons, duals, maps, *edges, observed)
    summed = sum_all(grad)
    r_edges = halos(C, resid, r_top, r_bottom)
    new_maps = call(functools.partial(corr_kernel, True), shape(M, ROWS, LANES), CORR_SCRATCH)(
        resid, *r_edges, filt, maps
    )
    new = call(
        last_kernel,
        [shape(M, FLAT)] * 3,
        [pltpu.VMEM((3, D_ROWS, LANES), F32), pltpu.VMEM((9 * M, WIDE), BF16)],
    )(summed, filt, cons, duals)
    return (new_maps, *new)


def solution(mesh):
    return jax.shard_map(
        local,
        mesh=mesh,
        in_specs=(P(None, "row", "col"), P(None, "row", "col"), P(), P(), P()),
        out_specs=(P(None, "row", "col"), P(), P(), P()),
        check_vma=False,
    )
```

```python
import functools
import math

import jax
import jax.numpy as jnp
from jax import lax
from jax.experimental import pallas as pl
from jax.experimental.pallas import tpu as pltpu
from jax.sharding import PartitionSpec as P

M = 96
C = 16
K = 7
REACH = 3
ITERS = 2
ROWS = 8
LANES = 128
PAD_ROWS = ROWS + 2 * REACH
TAPS = K * K
FLAT = C * TAPS
WIDE = K * LANES
D_ROWS = K * M
G_ROWS = 704
SLAB = 8 * M

step_coef = 0.5
sparsity = 0.1
dict_step = 0.08
penalty = 2.0
norm_scale = 1.0 / math.sqrt(M * K * K)

F32 = jnp.float32
BF16 = jnp.bfloat16


def shape(*dims):
    return jax.ShapeDtypeStruct(dims, F32)


def call(kernel, outs, scratch=()):
    return pl.pallas_call(
        kernel,
        out_shape=outs,
        scratch_shapes=list(scratch),
        compiler_params=pltpu.CompilerParams(vmem_limit_bytes=28 * 1024 * 1024),
    )


def split2(value):
    high = value.astype(BF16)
    return high, (value - high.astype(F32)).astype(BF16)


def split3(value):
    high = value.astype(BF16)
    rest = value - high.astype(F32)
    mid = rest.astype(BF16)
    return high, mid, (rest - mid.astype(F32)).astype(BF16)


def roll(value, shift):
    shift = shift % LANES
    return value if shift == 0 else pltpu.roll(value, shift, 1)


def lane_of(rows):
    return lax.broadcasted_iota(jnp.int32, (rows, LANES), 1)


def matmul(a, b):
    return jnp.dot(a, b, preferred_element_type=F32)


def matmul_nt(a, b):
    return lax.dot_general(a, b, (((1,), (1,)), ((), ())), preferred_element_type=F32)


def rows_kernel(maps, by_row, top, bottom):
    for y in range(ROWS):
        value = maps[:, y, :]
        by_row[y * M : (y + 1) * M, :] = value
        if y < REACH:
            top[y * M : (y + 1) * M, :] = value
        if y >= ROWS - REACH:
            at = (y - ROWS + REACH) * M
            bottom[at : at + M, :] = value


def flat_of(lane):
    row_tap = lane >> 7
    col_tap = (lane >> 4) & 7
    band = lane & 15
    return jnp.where(col_tap < K, band * TAPS + row_tap * K + col_tap, -1)


def to_rows_kernel(filt, cons, duals, filt_out, cons_out, duals_out, stacked):
    stacked[:, 6 * LANES :] = jnp.zeros((9 * M, LANES), BF16)
    for i, ref in enumerate((filt, cons, duals)):
        for j, part in enumerate(split3(ref[...])):
            at = (3 * i + j) * M
            stacked[at : at + M, :FLAT] = part
    source = lax.broadcasted_iota(jnp.int32, (WIDE, LANES), 0)
    lane = lane_of(WIDE)
    for a in range(K):
        pick = (source == flat_of(lane + a * LANES)).astype(F32).astype(BF16)
        moved = matmul(stacked[...], pick)
        for i, ref in enumerate((filt_out, cons_out, duals_out)):
            at = 3 * i * M
            ref[a * M : (a + 1) * M, :] = (
                moved[at : at + M] + moved[at + M : at + 2 * M] + moved[at + 2 * M : at + 3 * M]
            )


def padded_row(y, size, own, above, below):
    if y < REACH:
        return above[y * size : (y + 1) * size, :]
    if y < REACH + ROWS:
        at = (y - REACH) * size
        return own[at : at + size, :]
    at = (y - REACH - ROWS) * size
    return below[at : at + size, :]


def pack_kernel(size, own, above, below, left_edge, right_edge):
    lane = lane_of(size)
    left = jnp.zeros((size, LANES), F32)
    right = jnp.zeros((size, LANES), F32)
    for y in range(PAD_ROWS):
        value = padded_row(y, size, own, above, below)
        here = (lane >= 3 * y) & (lane < 3 * y + 3)
        left = jnp.where(here, roll(value, 3 * y), left)
        right = jnp.where(here, roll(value, 3 * y + 3), right)
    left_edge[...] = left
    right_edge[...] = right


def neighbours(axis, toward_high, toward_low):
    count = lax.axis_size(axis)
    up = [(i, i + 1) for i in range(count - 1)]
    down = [(i + 1, i) for i in range(count - 1)]
    return lax.ppermute(toward_high, axis, up), lax.ppermute(toward_low, axis, down)


def pack(size, own, above, below):
    return call(functools.partial(pack_kernel, size), [shape(size, LANES)] * 2)(own, above, below)


def halos(size, own, top, bottom):
    above, below = neighbours("row", bottom, top)
    left_edge, right_edge = pack(size, own, above, below)
    left, right = neighbours("col", right_edge, left_edge)
    return above, below, left, right


def recon_and_grad(
    maps, above, below, left, right, observed, filt,
    resid_out, top, bottom, grad, x_hi, x_lo, h_hi, h_lo, r_all, r_edge,
):
    for y in range(PAD_ROWS):
        hi, lo = split2(padded_row(y, M, maps, above, below))
        for ref, part in ((x_hi, hi), (x_lo, lo)):
            ref[y * M : (y + 1) * M, :LANES] = part
            if y > 0:
                ref[(y - 1) * M : y * M, LANES:] = part
    for ref in (x_hi, x_lo):
        ref[(PAD_ROWS - 1) * M :, LANES:] = jnp.zeros((M, LANES), BF16)
    edge = jnp.where(lane_of(M) < 64, right[...], roll(left[...], 64))
    for a in range(K):
        hi, lo = split2(roll(edge, -3 * a))
        h_hi[a * M : (a + 1) * M, :] = hi
        h_lo[a * M : (a + 1) * M, :] = lo
    for ref in (h_hi, h_lo):
        ref[D_ROWS:, :] = jnp.zeros((SLAB - D_ROWS, LANES), BF16)

    turned = jnp.concatenate([filt, jnp.zeros((SLAB - D_ROWS, LANES), F32)], axis=0).T
    d_hi, d_lo = split2(turned)
    d_both = jnp.concatenate([d_hi, d_lo], axis=0)

    def apply(hi, lo):
        both = matmul(d_both, hi)
        return both[:LANES] + both[LANES:] + matmul(d_hi, lo)

    lane = lane_of(C)
    at_edge = apply(h_hi[...], h_lo[...])
    resid = []
    for y in range(0, ROWS, 2):
        planes = apply(x_hi[y * M : y * M + SLAB, :], x_lo[y * M : y * M + SLAB, :])
        for k in range(2):
            row = y + k
            total = jnp.zeros((C, LANES), F32)
            for b in range(K):
                d = b - REACH
                own = roll(planes[b * C : (b + 1) * C, k * LANES : (k + 1) * LANES], -d)
                band_edge = at_edge[b * C : (b + 1) * C, :]
                if d > 0:
                    moved = roll(band_edge, 131 - b - 3 * row)
                    own = jnp.where(lane >= LANES - d, moved, own)
                elif d < 0:
                    moved = roll(band_edge, -(64 + 3 * row) - b)
                    own = jnp.where(lane < -d, moved, own)
                total = total + own
            value = norm_scale * total - observed[:, row, :]
            resid.append(value)
            resid_out[row * C : (row + 1) * C, :] = value
            if row < REACH:
                top[row * C : (row + 1) * C, :] = value
            if row >= ROWS - REACH:
                at = (row - ROWS + REACH) * C
                bottom[at : at + C, :] = value

    zero16 = jnp.zeros((C, LANES), F32)
    for b in range(K):
        d = b - REACH
        near = zero16
        for row in range(ROWS):
            moved = roll(resid[row], d)
            if d > 0:
                moved = jnp.where(lane >= d, moved, 0.0)
                here = (lane >= 3 * row) & (lane < 3 * row + d)
                near = jnp.where(here, roll(resid[row], 3 * row - 131 + b), near)
            elif d < 0:
                moved = jnp.where(lane < LANES + d, moved, 0.0)
                here = (lane >= 64 + 3 * row + b) & (lane < 64 + 3 * row + 3)
                near = jnp.where(here, roll(resid[row], 64 + 3 * row + b), near)
            hi, lo = split2(moved)
            r_all[b * C : (b + 1) * C, row * LANES : (row + 1) * LANES] = hi
            r_all[LANES + b * C : LANES + (b + 1) * C, row * LANES : (row + 1) * LANES] = lo
        hi, lo = split2(near)
        r_edge[b * C : (b + 1) * C, :] = hi
        r_edge[LANES + b * C : LANES + (b + 1) * C, :] = lo
    for at in (K * C, LANES + K * C):
        r_all[at : at + C, :] = jnp.zeros((C, ROWS * LANES), BF16)
        r_edge[at : at + C, :] = jnp.zeros((C, LANES), BF16)

    def gather(hi, lo, spread):
        both = matmul_nt(hi, spread)
        return both[:, :LANES] + both[:, LANES:] + matmul_nt(lo, spread[:LANES])

    total = gather(h_hi[:D_ROWS, :], h_lo[:D_ROWS, :], r_edge[...])
    for y in range(0, ROWS, 2):
        total = total + gather(
            x_hi[y * M : y * M + D_ROWS, :],
            x_lo[y * M : y * M + D_ROWS, :],
            r_all[:, y * LANES : (y + 2) * LANES],
        )
    grad[:D_ROWS, :] = total
    grad[D_ROWS:, :] = jnp.zeros((G_ROWS - D_ROWS, LANES), F32)


RECON_OUT = [shape(ROWS * C, LANES), shape(3 * C, LANES), shape(3 * C, LANES), shape(G_ROWS, LANES)]
RECON_SCRATCH = [
    pltpu.VMEM((PAD_ROWS * M, 2 * LANES), BF16),
    pltpu.VMEM((PAD_ROWS * M, 2 * LANES), BF16),
    pltpu.VMEM((SLAB, LANES), BF16),
    pltpu.VMEM((SLAB, LANES), BF16),
    pltpu.VMEM((2 * LANES, ROWS * LANES), BF16),
    pltpu.VMEM((2 * LANES, LANES), BF16),
]


def updated(summed, filt, cons, duals, keep):
    squares = jnp.zeros((M, LANES), F32)
    for a in range(K):
        at = slice(a * M, (a + 1) * M)
        now, dual = filt[at, :], duals[at, :]
        after = now - dict_step * (norm_scale * summed[at, :] + penalty * (now - cons[at, :] + dual))
        joined = after + dual
        squares = squares + joined * joined
        keep(0, a, after)
        keep(1, a, joined)
    spread = jnp.sqrt(jnp.sum(squares, axis=1, keepdims=True) / FLAT)
    return 1.0 / jnp.maximum(1.0, spread)


def first_kernel(maps, above, below, left, right, observed, filt, *rest):
    recon_and_grad(maps, above, below, left, right, observed, filt[...], *rest)


def next_kernel(
    summed, filt, cons, duals, maps, above, below, left, right, observed,
    filt_out, cons_out, duals_out, *rest,
):
    update_into(summed, filt, cons, duals, filt_out, cons_out, duals_out)
    recon_and_grad(maps, above, below, left, right, observed, filt_out[...], *rest)


def update_into(summed, filt, cons, duals, filt_out, cons_out, duals_out):
    refs = (filt_out, cons_out)

    def keep(which, a, value):
        refs[which][a * M : (a + 1) * M, :] = value

    factor = updated(summed, filt, cons, duals, keep)
    for a in range(K):
        at = slice(a * M, (a + 1) * M)
        joined = cons_out[at, :]
        projected = joined * factor
        cons_out[at, :] = projected
        duals_out[at, :] = joined - projected


def last_kernel(summed, filt, cons, duals, filt_out, cons_out, duals_out, new, stacked):
    update_into(summed, filt, cons, duals, new.at[0], new.at[1], new.at[2])
    for i in range(3):
        for a in range(K):
            for j, part in enumerate(split3(new[i, a * M : (a + 1) * M, :])):
                at = (3 * i + j) * M
                stacked[at : at + M, a * LANES : (a + 1) * LANES] = part
    source = lax.broadcasted_iota(jnp.int32, (WIDE, LANES), 0)
    wanted = flat_of(source)
    for block in range(K):
        target = lane_of(WIDE) + block * LANES
        pick = (wanted == target).astype(F32).astype(BF16)
        moved = matmul(stacked[...], pick)
        width = min(LANES, FLAT - block * LANES)
        for i, ref in enumerate((filt_out, cons_out, duals_out)):
            at = 3 * i * M
            value = moved[at : at + M] + moved[at + M : at + 2 * M] + moved[at + 2 * M : at + 3 * M]
            ref[:, block * LANES : block * LANES + width] = value[:, :width]


def corr_kernel(last, resid, above, below, left, right, filt, maps, *rest):
    if last:
        maps_out, s_hi, s_lo = rest
    else:
        maps_out, top, bottom, s_hi, s_lo = rest
    lane = lane_of(C)
    for y in range(PAD_ROWS - 1 + 1):
        own = padded_row(y, C, resid, above, below)
        edge = jnp.where(lane < 3, roll(right[...], -3 * y), roll(left[...], 125 - 3 * y))
        for b in range(K + 1):
            if b < K:
                d = b - REACH
                value = own
                if d > 0:
                    value = jnp.where(lane >= LANES - d, edge, own)
                elif d < 0:
                    value = jnp.where(lane < -d, edge, own)
                hi, lo = split2(roll(value, d))
            else:
                hi = lo = jnp.zeros((C, LANES), BF16)
            for ref, part in ((s_hi, hi), (s_lo, lo)):
                at = y * LANES + b * C
                if y < PAD_ROWS - 1:
                    ref[at : at + C, :LANES] = part
                if y > 0:
                    ref[at - LANES : at - LANES + C, LANES:] = part

    across = jnp.concatenate([filt[(6 - q) * M : (7 - q) * M, :] for q in range(K)], axis=1)
    d_hi, d_lo = split2(across)
    d_both = jnp.concatenate([d_hi, d_lo], axis=0)
    limit = step_coef * sparsity
    for y in range(0, ROWS, 2):
        slab = slice(y * LANES, y * LANES + WIDE)
        both = matmul(d_both, s_hi[slab, :])
        corr = both[:M] + both[M:] + matmul(d_hi, s_lo[slab, :])
        for k in range(2):
            row = y + k
            moved = maps[row * M : (row + 1) * M, :] - (step_coef * norm_scale) * corr[
                :, k * LANES : (k + 1) * LANES
            ]
            value = moved - jnp.clip(moved, -limit, limit)
            if last:
                maps_out[:, row, :] = value
                continue
            maps_out[row * M : (row + 1) * M, :] = value
            if row < REACH:
                top[row * M : (row + 1) * M, :] = value
            if row >= ROWS - REACH:
                at = (row - ROWS + REACH) * M
                bottom[at : at + M, :] = value


CORR_SCRATCH = [pltpu.VMEM(((PAD_ROWS - 1) * LANES, 2 * LANES), BF16)] * 2


def swap_even(i):
    return i ^ 1


def swap_odd(i, count):
    return (i + 1) % count if i % 2 == 1 else (i - 1) % count


THIRD = {2: 5, 5: 2, 1: 6, 6: 1, 3: 0, 0: 3, 4: 7, 7: 4}
INWARD = [(2 * y, 2 * y + 1) for y in range(4)]
OUTWARD = [(2 * y + 1, 2 * y) for y in range(4)]
Y_EVEN = [(2 * y + 1, 2 * swap_even(y) + 1) for y in range(4)]
Y_ODD = [(2 * y + 1, 2 * swap_odd(y, 4) + 1) for y in range(4)]


def pairs_col(change):
    pairs = [(8 * x + z, change(x, z)) for x in range(4) for z in range(8)]
    return [(32 * row + i, 32 * row + j) for row in (1, 3, 5, 7) for i, j in pairs]


COLS = [
    pairs_col(lambda x, z: swap_even(x) * 8 + z),
    pairs_col(lambda x, z: swap_odd(x, 4) * 8 + z),
    pairs_col(lambda x, z: x * 8 + swap_even(z)),
    pairs_col(lambda x, z: x * 8 + swap_odd(z, 8)),
    pairs_col(lambda x, z: x * 8 + THIRD[z]),
]


def halves(value, bit):
    half = value.shape[0] // 2
    low, high = value[:half], value[half:]
    return jnp.where(bit, low, high), jnp.where(bit, high, low)


def joined(mine, other, bit):
    return jnp.where(bit, jnp.concatenate([other, mine]), jnp.concatenate([mine, other]))


def sum_all(grad, state, side):
    row = lax.axis_index("row")
    y = row // 2
    upper = (y == 1) | (y == 2)
    later = (y == 2) | (y == 3)
    value = grad

    def beside(k, sent, axes, pairs, kept):
        nonlocal state
        sent, kept, state = lax.optimization_barrier((sent, kept, state))
        other = lax.ppermute(sent, axes, pairs)
        if k in side:
            state = side[k](state)
        return kept, other

    kept, other = beside(0, value, "row", INWARD, value)
    value = kept + other
    for k, bit, pairs in ((1, upper, Y_EVEN), (2, later, Y_ODD)):
        sent, kept = halves(value, bit)
        kept, other = beside(k, sent, "row", pairs, kept)
        value = kept + other
    for k, pairs in enumerate(COLS):
        kept, other = beside(3 + k, value, ("row", "col"), pairs, value)
        value = kept + other
    for k, bit, pairs in ((8, later, Y_ODD), (9, upper, Y_EVEN)):
        kept, other = beside(k, value, "row", pairs, value)
        value = joined(kept, other, bit)
    kept, other = beside(10, value, "row", OUTWARD, value)
    return jnp.where(row % 2 == 0, other, kept), state


def local(observed, coef_maps, dictionary, consensus, dual_vars):
    map_rows = [shape(ROWS * M, LANES), shape(3 * M, LANES), shape(3 * M, LANES)]
    filters = [shape(D_ROWS, LANES)] * 3
    maps, top, bottom = call(rows_kernel, map_rows)(coef_maps)
    filt, cons, duals = call(to_rows_kernel, filters, [pltpu.VMEM((9 * M, WIDE), BF16)])(
        dictionary, consensus, dual_vars
    )
    edges = halos(M, maps, top, bottom)
    resid, r_top, r_bottom, grad = call(first_kernel, RECON_OUT, RECON_SCRATCH)(
        maps, *edges, observed, filt
    )

    def resid_rows(state):
        resid, top, bottom, filt, maps = state
        return resid, neighbours("row", bottom, top), filt, maps

    def resid_columns(state):
        resid, around, filt, maps = state
        left_edge, right_edge = pack(C, resid, *around)
        return resid, (*around, *neighbours("col", right_edge, left_edge)), filt, maps

    def threshold(last, outs):
        def run(state):
            resid, around, filt, maps = state
            return call(functools.partial(corr_kernel, last), outs, CORR_SCRATCH)(
                resid, *around, filt, maps
            )

        return run

    def map_rows_out(state):
        maps, top, bottom = state
        return maps, neighbours("row", bottom, top)

    def map_pack(state):
        maps, around = state
        return maps, around, pack(M, maps, *around)

    def map_columns(state):
        maps, around, (left_edge, right_edge) = state
        return maps, (*around, *neighbours("col", right_edge, left_edge))

    summed, (maps, edges) = sum_all(
        grad,
        (resid, r_top, r_bottom, filt, maps),
        {
            0: resid_rows,
            1: resid_columns,
            2: threshold(False, map_rows),
            3: map_rows_out,
            5: map_pack,
            8: map_columns,
        },
    )
    filt, cons, duals, resid, r_top, r_bottom, grad = call(
        next_kernel, filters + RECON_OUT, RECON_SCRATCH
    )(summed, filt, cons, duals, maps, *edges, observed)
    summed, new_maps = sum_all(
        grad,
        (resid, r_top, r_bottom, filt, maps),
        {0: resid_rows, 3: resid_columns, 5: threshold(True, shape(M, ROWS, LANES))},
    )
    new = call(
        last_kernel,
        [shape(M, FLAT)] * 3,
        [pltpu.VMEM((3, D_ROWS, LANES), F32), pltpu.VMEM((9 * M, WIDE), BF16)],
    )(summed, filt, cons, duals)
    return (new_maps, *new)


def solution(mesh):
    return jax.shard_map(
        local,
        mesh=mesh,
        in_specs=(P(None, "row", "col"), P(None, "row", "col"), P(), P(), P()),
        out_specs=(P(None, "row", "col"), P(), P(), P()),
        check_vma=False,
    )
```

```python
import functools
import math

import jax
import jax.numpy as jnp
from jax import lax
from jax.experimental import pallas as pl
from jax.experimental.pallas import tpu as pltpu
from jax.sharding import PartitionSpec as P

M = 96
C = 16
K = 7
REACH = 3
ITERS = 2
ROWS = 8
LANES = 128
PAD_ROWS = ROWS + 2 * REACH
TAPS = K * K
FLAT = C * TAPS
WIDE = K * LANES
D_ROWS = K * M
G_ROWS = 704
SLAB = 8 * M

step_coef = 0.5
sparsity = 0.1
dict_step = 0.08
penalty = 2.0
norm_scale = 1.0 / math.sqrt(M * K * K)

F32 = jnp.float32
BF16 = jnp.bfloat16


def shape(*dims):
    return jax.ShapeDtypeStruct(dims, F32)


def call(kernel, outs, scratch=()):
    return pl.pallas_call(
        kernel,
        out_shape=outs,
        scratch_shapes=list(scratch),
        compiler_params=pltpu.CompilerParams(vmem_limit_bytes=28 * 1024 * 1024),
    )


def split2(value):
    high = value.astype(BF16)
    return high, (value - high.astype(F32)).astype(BF16)


def split3(value):
    high = value.astype(BF16)
    rest = value - high.astype(F32)
    mid = rest.astype(BF16)
    return high, mid, (rest - mid.astype(F32)).astype(BF16)


def roll(value, shift):
    shift = shift % LANES
    return value if shift == 0 else pltpu.roll(value, shift, 1)


def lane_of(rows):
    return lax.broadcasted_iota(jnp.int32, (rows, LANES), 1)


def matmul(a, b):
    return jnp.dot(a, b, preferred_element_type=F32)


def matmul_nt(a, b):
    return lax.dot_general(a, b, (((1,), (1,)), ((), ())), preferred_element_type=F32)


def rows_kernel(maps, by_row, top, bottom):
    for y in range(ROWS):
        value = maps[:, y, :]
        by_row[y * M : (y + 1) * M, :] = value
        if y < REACH:
            top[y * M : (y + 1) * M, :] = value
        if y >= ROWS - REACH:
            at = (y - ROWS + REACH) * M
            bottom[at : at + M, :] = value


def flat_of(lane):
    row_tap = lane >> 7
    col_tap = (lane >> 4) & 7
    band = lane & 15
    return jnp.where(col_tap < K, band * TAPS + row_tap * K + col_tap, -1)


def to_rows_kernel(filt, cons, duals, filt_out, cons_out, duals_out, stacked):
    stacked[:, 6 * LANES :] = jnp.zeros((9 * M, LANES), BF16)
    for i, ref in enumerate((filt, cons, duals)):
        for j, part in enumerate(split3(ref[...])):
            at = (3 * i + j) * M
            stacked[at : at + M, :FLAT] = part
    source = lax.broadcasted_iota(jnp.int32, (WIDE, LANES), 0)
    lane = lane_of(WIDE)
    for a in range(K):
        pick = (source == flat_of(lane + a * LANES)).astype(F32).astype(BF16)
        moved = matmul(stacked[...], pick)
        for i, ref in enumerate((filt_out, cons_out, duals_out)):
            at = 3 * i * M
            ref[a * M : (a + 1) * M, :] = (
                moved[at : at + M] + moved[at + M : at + 2 * M] + moved[at + 2 * M : at + 3 * M]
            )


def padded_row(y, size, own, above, below):
    if y < REACH:
        return above[y * size : (y + 1) * size, :]
    if y < REACH + ROWS:
        at = (y - REACH) * size
        return own[at : at + size, :]
    at = (y - REACH - ROWS) * size
    return below[at : at + size, :]


def pack_kernel(size, own, above, below, left_edge, right_edge):
    lane = lane_of(size)
    left = jnp.zeros((size, LANES), F32)
    right = jnp.zeros((size, LANES), F32)
    for y in range(PAD_ROWS):
        value = padded_row(y, size, own, above, below)
        here = (lane >= 3 * y) & (lane < 3 * y + 3)
        left = jnp.where(here, roll(value, 3 * y), left)
        right = jnp.where(here, roll(value, 3 * y + 3), right)
    left_edge[...] = left
    right_edge[...] = right


def neighbours(axis, toward_high, toward_low):
    count = lax.axis_size(axis)
    up = [(i, i + 1) for i in range(count - 1)]
    down = [(i + 1, i) for i in range(count - 1)]
    return lax.ppermute(toward_high, axis, up), lax.ppermute(toward_low, axis, down)


def pack(size, own, above, below):
    return call(functools.partial(pack_kernel, size), [shape(size, LANES)] * 2)(own, above, below)


def halos(size, own, top, bottom):
    above, below = neighbours("row", bottom, top)
    left_edge, right_edge = pack(size, own, above, below)
    left, right = neighbours("col", right_edge, left_edge)
    return above, below, left, right


def recon_and_grad(
    maps, above, below, left, right, observed, filt,
    resid_out, top, bottom, grad, x_hi, x_lo, h_hi, h_lo, r_all, r_edge,
):
    for y in range(PAD_ROWS):
        hi, lo = split2(padded_row(y, M, maps, above, below))
        for ref, part in ((x_hi, hi), (x_lo, lo)):
            ref[y * M : (y + 1) * M, :LANES] = part
            if y > 0:
                ref[(y - 1) * M : y * M, LANES:] = part
    for ref in (x_hi, x_lo):
        ref[(PAD_ROWS - 1) * M :, LANES:] = jnp.zeros((M, LANES), BF16)
    edge = jnp.where(lane_of(M) < 64, right[...], roll(left[...], 64))
    for a in range(K):
        hi, lo = split2(roll(edge, -3 * a))
        h_hi[a * M : (a + 1) * M, :] = hi
        h_lo[a * M : (a + 1) * M, :] = lo
    for ref in (h_hi, h_lo):
        ref[D_ROWS:, :] = jnp.zeros((SLAB - D_ROWS, LANES), BF16)

    turned = jnp.concatenate([filt, jnp.zeros((SLAB - D_ROWS, LANES), F32)], axis=0).T
    d_hi, d_lo = split2(turned)
    d_both = jnp.concatenate([d_hi, d_lo], axis=0)

    def apply(hi, lo):
        both = matmul(d_both, hi)
        return both[:LANES] + both[LANES:] + matmul(d_hi, lo)

    lane = lane_of(C)
    at_edge = apply(h_hi[...], h_lo[...])
    resid = []
    for y in range(0, ROWS, 2):
        planes = apply(x_hi[y * M : y * M + SLAB, :], x_lo[y * M : y * M + SLAB, :])
        for k in range(2):
            row = y + k
            total = jnp.zeros((C, LANES), F32)
            for b in range(K):
                d = b - REACH
                own = roll(planes[b * C : (b + 1) * C, k * LANES : (k + 1) * LANES], -d)
                band_edge = at_edge[b * C : (b + 1) * C, :]
                if d > 0:
                    moved = roll(band_edge, 131 - b - 3 * row)
                    own = jnp.where(lane >= LANES - d, moved, own)
                elif d < 0:
                    moved = roll(band_edge, -(64 + 3 * row) - b)
                    own = jnp.where(lane < -d, moved, own)
                total = total + own
            value = norm_scale * total - observed[:, row, :]
            resid.append(value)
            resid_out[row * C : (row + 1) * C, :] = value
            if row < REACH:
                top[row * C : (row + 1) * C, :] = value
            if row >= ROWS - REACH:
                at = (row - ROWS + REACH) * C
                bottom[at : at + C, :] = value

    zero16 = jnp.zeros((C, LANES), F32)
    for b in range(K):
        d = b - REACH
        near = zero16
        for row in range(ROWS):
            moved = roll(resid[row], d)
            if d > 0:
                moved = jnp.where(lane >= d, moved, 0.0)
                here = (lane >= 3 * row) & (lane < 3 * row + d)
                near = jnp.where(here, roll(resid[row], 3 * row - 131 + b), near)
            elif d < 0:
                moved = jnp.where(lane < LANES + d, moved, 0.0)
                here = (lane >= 64 + 3 * row + b) & (lane < 64 + 3 * row + 3)
                near = jnp.where(here, roll(resid[row], 64 + 3 * row + b), near)
            hi, lo = split2(moved)
            r_all[b * C : (b + 1) * C, row * LANES : (row + 1) * LANES] = hi
            r_all[LANES + b * C : LANES + (b + 1) * C, row * LANES : (row + 1) * LANES] = lo
        hi, lo = split2(near)
        r_edge[b * C : (b + 1) * C, :] = hi
        r_edge[LANES + b * C : LANES + (b + 1) * C, :] = lo
    for at in (K * C, LANES + K * C):
        r_all[at : at + C, :] = jnp.zeros((C, ROWS * LANES), BF16)
        r_edge[at : at + C, :] = jnp.zeros((C, LANES), BF16)

    def gather(hi, lo, spread):
        both = matmul_nt(hi, spread)
        return both[:, :LANES] + both[:, LANES:] + matmul_nt(lo, spread[:LANES])

    total = gather(h_hi[:D_ROWS, :], h_lo[:D_ROWS, :], r_edge[...])
    for y in range(0, ROWS, 2):
        total = total + gather(
            x_hi[y * M : y * M + D_ROWS, :],
            x_lo[y * M : y * M + D_ROWS, :],
            r_all[:, y * LANES : (y + 2) * LANES],
        )
    grad[:D_ROWS, :] = total
    grad[D_ROWS:, :] = jnp.zeros((G_ROWS - D_ROWS, LANES), F32)


RECON_OUT = [shape(ROWS * C, LANES), shape(3 * C, LANES), shape(3 * C, LANES), shape(G_ROWS, LANES)]
RECON_SCRATCH = [
    pltpu.VMEM((PAD_ROWS * M, 2 * LANES), BF16),
    pltpu.VMEM((PAD_ROWS * M, 2 * LANES), BF16),
    pltpu.VMEM((SLAB, LANES), BF16),
    pltpu.VMEM((SLAB, LANES), BF16),
    pltpu.VMEM((2 * LANES, ROWS * LANES), BF16),
    pltpu.VMEM((2 * LANES, LANES), BF16),
]


def updated(summed, filt, cons, duals, keep):
    squares = jnp.zeros((M, LANES), F32)
    for a in range(K):
        at = slice(a * M, (a + 1) * M)
        now, dual = filt[at, :], duals[at, :]
        after = now - dict_step * (norm_scale * summed[at, :] + penalty * (now - cons[at, :] + dual))
        joined = after + dual
        squares = squares + joined * joined
        keep(0, a, after)
        keep(1, a, joined)
    spread = jnp.sqrt(jnp.sum(squares, axis=1, keepdims=True) / FLAT)
    return 1.0 / jnp.maximum(1.0, spread)


def first_kernel(maps, above, below, left, right, observed, filt, *rest):
    recon_and_grad(maps, above, below, left, right, observed, filt[...], *rest)


def next_kernel(
    summed, filt, cons, duals, maps, above, below, left, right, observed,
    filt_out, cons_out, duals_out, *rest,
):
    update_into(summed, filt, cons, duals, filt_out, cons_out, duals_out)
    recon_and_grad(maps, above, below, left, right, observed, filt_out[...], *rest)


def update_into(summed, filt, cons, duals, filt_out, cons_out, duals_out):
    refs = (filt_out, cons_out)

    def keep(which, a, value):
        refs[which][a * M : (a + 1) * M, :] = value

    factor = updated(summed, filt, cons, duals, keep)
    for a in range(K):
        at = slice(a * M, (a + 1) * M)
        joined = cons_out[at, :]
        projected = joined * factor
        cons_out[at, :] = projected
        duals_out[at, :] = joined - projected


def last_kernel(summed, filt, cons, duals, filt_out, cons_out, duals_out, new, stacked):
    update_into(summed, filt, cons, duals, new.at[0], new.at[1], new.at[2])
    for i in range(3):
        for a in range(K):
            for j, part in enumerate(split3(new[i, a * M : (a + 1) * M, :])):
                at = (3 * i + j) * M
                stacked[at : at + M, a * LANES : (a + 1) * LANES] = part
    source = lax.broadcasted_iota(jnp.int32, (WIDE, LANES), 0)
    wanted = flat_of(source)
    for block in range(K):
        target = lane_of(WIDE) + block * LANES
        pick = (wanted == target).astype(F32).astype(BF16)
        moved = matmul(stacked[...], pick)
        width = min(LANES, FLAT - block * LANES)
        for i, ref in enumerate((filt_out, cons_out, duals_out)):
            at = 3 * i * M
            value = moved[at : at + M] + moved[at + M : at + 2 * M] + moved[at + 2 * M : at + 3 * M]
            ref[:, block * LANES : block * LANES + width] = value[:, :width]


def corr_kernel(last, resid, above, below, left, right, filt, maps, *rest):
    if last:
        maps_out, s_hi, s_lo = rest
    else:
        maps_out, top, bottom, s_hi, s_lo = rest
    lane = lane_of(C)
    for y in range(PAD_ROWS - 1 + 1):
        own = padded_row(y, C, resid, above, below)
        edge = jnp.where(lane < 3, roll(right[...], -3 * y), roll(left[...], 125 - 3 * y))
        for b in range(K + 1):
            if b < K:
                d = b - REACH
                value = own
                if d > 0:
                    value = jnp.where(lane >= LANES - d, edge, own)
                elif d < 0:
                    value = jnp.where(lane < -d, edge, own)
                hi, lo = split2(roll(value, d))
            else:
                hi = lo = jnp.zeros((C, LANES), BF16)
            for ref, part in ((s_hi, hi), (s_lo, lo)):
                at = y * LANES + b * C
                if y < PAD_ROWS - 1:
                    ref[at : at + C, :LANES] = part
                if y > 0:
                    ref[at - LANES : at - LANES + C, LANES:] = part

    across = jnp.concatenate([filt[(6 - q) * M : (7 - q) * M, :] for q in range(K)], axis=1)
    d_hi, d_lo = split2(across)
    d_both = jnp.concatenate([d_hi, d_lo], axis=0)
    limit = step_coef * sparsity
    for y in range(0, ROWS, 2):
        slab = slice(y * LANES, y * LANES + WIDE)
        both = matmul(d_both, s_hi[slab, :])
        corr = both[:M] + both[M:] + matmul(d_hi, s_lo[slab, :])
        for k in range(2):
            row = y + k
            moved = maps[row * M : (row + 1) * M, :] - (step_coef * norm_scale) * corr[
                :, k * LANES : (k + 1) * LANES
            ]
            value = moved - jnp.clip(moved, -limit, limit)
            if last:
                maps_out[:, row, :] = value
                continue
            maps_out[row * M : (row + 1) * M, :] = value
            if row < REACH:
                top[row * M : (row + 1) * M, :] = value
            if row >= ROWS - REACH:
                at = (row - ROWS + REACH) * M
                bottom[at : at + M, :] = value


CORR_SCRATCH = [pltpu.VMEM(((PAD_ROWS - 1) * LANES, 2 * LANES), BF16)] * 2


def swap_even(i):
    return i ^ 1


def swap_odd(i, count):
    return (i + 1) % count if i % 2 == 1 else (i - 1) % count


THIRD = {2: 5, 5: 2, 1: 6, 6: 1, 3: 0, 0: 3, 4: 7, 7: 4}
CORE = [(i, i ^ 1) for i in range(8)]
Y_EVEN = [(2 * y + core, 2 * swap_even(y) + core) for y in range(4) for core in range(2)]
Y_ODD = [(2 * y + core, 2 * swap_odd(y, 4) + core) for y in range(4) for core in range(2)]


def pairs_col(change):
    return [(8 * x + z, change(x, z)) for x in range(4) for z in range(8)]


COLS = [
    pairs_col(lambda x, z: swap_even(x) * 8 + z),
    pairs_col(lambda x, z: swap_odd(x, 4) * 8 + z),
    pairs_col(lambda x, z: x * 8 + swap_even(z)),
    pairs_col(lambda x, z: x * 8 + swap_odd(z, 8)),
    pairs_col(lambda x, z: x * 8 + THIRD[z]),
]


def halves(value, bit):
    half = value.shape[0] // 2
    low, high = value[:half], value[half:]
    return jnp.where(bit, low, high), jnp.where(bit, high, low)


def joined(mine, other, bit):
    return jnp.where(bit, jnp.concatenate([other, mine]), jnp.concatenate([mine, other]))


def sum_all(grad, state, side):
    row = lax.axis_index("row")
    y = row // 2
    upper = (y == 1) | (y == 2)
    odd_core = row % 2 == 1
    value = grad

    def beside(k, sent, axis, pairs, kept):
        nonlocal state
        sent, kept, state = lax.optimization_barrier((sent, kept, state))
        other = lax.ppermute(sent, axis, pairs)
        if k in side:
            state = side[k](state)
        return kept, other

    for k, bit, pairs in ((0, odd_core, CORE), (1, upper, Y_EVEN)):
        sent, kept = halves(value, bit)
        kept, other = beside(k, sent, "row", pairs, kept)
        value = kept + other
    steps = [("row", Y_ODD)] + [("col", pairs) for pairs in COLS]
    for k, (axis, pairs) in enumerate(steps):
        kept, other = beside(2 + k, value, axis, pairs, value)
        value = kept + other
    for k, bit, pairs in ((8, upper, Y_EVEN), (9, odd_core, CORE)):
        kept, other = beside(k, value, "row", pairs, value)
        value = joined(kept, other, bit)
    return value, state


def local(observed, coef_maps, dictionary, consensus, dual_vars):
    map_rows = [shape(ROWS * M, LANES), shape(3 * M, LANES), shape(3 * M, LANES)]
    filters = [shape(D_ROWS, LANES)] * 3
    maps, top, bottom = call(rows_kernel, map_rows)(coef_maps)
    filt, cons, duals = call(to_rows_kernel, filters, [pltpu.VMEM((9 * M, WIDE), BF16)])(
        dictionary, consensus, dual_vars
    )
    edges = halos(M, maps, top, bottom)
    resid, r_top, r_bottom, grad = call(first_kernel, RECON_OUT, RECON_SCRATCH)(
        maps, *edges, observed, filt
    )

    def resid_rows(state):
        resid, top, bottom, filt, maps = state
        return resid, neighbours("row", bottom, top), filt, maps

    def resid_columns(state):
        resid, around, filt, maps = state
        left_edge, right_edge = pack(C, resid, *around)
        return resid, (*around, *neighbours("col", right_edge, left_edge)), filt, maps

    def threshold(last, outs):
        def run(state):
            resid, around, filt, maps = state
            return call(functools.partial(corr_kernel, last), outs, CORR_SCRATCH)(
                resid, *around, filt, maps
            )

        return run

    def map_rows_out(state):
        maps, top, bottom = state
        return maps, neighbours("row", bottom, top)

    def map_pack(state):
        maps, around = state
        return maps, around, pack(M, maps, *around)

    def map_columns(state):
        maps, around, (left_edge, right_edge) = state
        return maps, (*around, *neighbours("col", right_edge, left_edge))

    summed, (maps, edges) = sum_all(
        grad,
        (resid, r_top, r_bottom, filt, maps),
        {
            0: resid_rows,
            1: resid_columns,
            2: threshold(False, map_rows),
            3: map_rows_out,
            5: map_pack,
            7: map_columns,
        },
    )
    filt, cons, duals, resid, r_top, r_bottom, grad = call(
        next_kernel, filters + RECON_OUT, RECON_SCRATCH
    )(summed, filt, cons, duals, maps, *edges, observed)
    summed, new_maps = sum_all(
        grad,
        (resid, r_top, r_bottom, filt, maps),
        {2: resid_rows, 7: resid_columns, 8: threshold(True, shape(M, ROWS, LANES))},
    )
    new = call(
        last_kernel,
        [shape(M, FLAT)] * 3,
        [pltpu.VMEM((3, D_ROWS, LANES), F32), pltpu.VMEM((9 * M, WIDE), BF16)],
    )(summed, filt, cons, duals)
    return (new_maps, *new)


def solution(mesh):
    return jax.shard_map(
        local,
        mesh=mesh,
        in_specs=(P(None, "row", "col"), P(None, "row", "col"), P(), P(), P()),
        out_specs=(P(None, "row", "col"), P(), P(), P()),
        check_vma=False,
    )
```

```python
import functools
import math

import jax
import jax.numpy as jnp
from jax import lax
from jax.experimental import pallas as pl
from jax.experimental.pallas import tpu as pltpu
from jax.sharding import PartitionSpec as P

M = 96
C = 16
K = 7
REACH = 3
ITERS = 2
ROWS = 8
LANES = 128
PAD_ROWS = ROWS + 2 * REACH
TAPS = K * K
FLAT = C * TAPS
WIDE = K * LANES
D_ROWS = K * M
G_ROWS = D_ROWS
SLAB = 8 * M

step_coef = 0.5
sparsity = 0.1
dict_step = 0.08
penalty = 2.0
norm_scale = 1.0 / math.sqrt(M * K * K)

F32 = jnp.float32
BF16 = jnp.bfloat16


def shape(*dims):
    return jax.ShapeDtypeStruct(dims, F32)


def call(kernel, outs, scratch=()):
    return pl.pallas_call(
        kernel,
        out_shape=outs,
        scratch_shapes=list(scratch),
        compiler_params=pltpu.CompilerParams(vmem_limit_bytes=28 * 1024 * 1024),
    )


def split2(value):
    high = value.astype(BF16)
    return high, (value - high.astype(F32)).astype(BF16)


def roll(value, shift):
    shift = shift % LANES
    return value if shift == 0 else pltpu.roll(value, shift, 1)


def lane_of(rows):
    return lax.broadcasted_iota(jnp.int32, (rows, LANES), 1)


def matmul(a, b):
    return jnp.dot(a, b, preferred_element_type=F32)


def matmul_nt(a, b):
    return lax.dot_general(a, b, (((1,), (1,)), ((), ())), preferred_element_type=F32)


def rows_kernel(maps, by_row, top, bottom):
    for y in range(ROWS):
        value = maps[:, y, :]
        by_row[y * M : (y + 1) * M, :] = value
        if y < REACH:
            top[y * M : (y + 1) * M, :] = value
        if y >= ROWS - REACH:
            at = (y - ROWS + REACH) * M
            bottom[at : at + M, :] = value


def flat_of(lane):
    row_tap = lane >> 7
    col_tap = (lane >> 4) & 7
    band = lane & 15
    return jnp.where(col_tap < K, band * TAPS + row_tap * K + col_tap, -1)


def to_rows_kernel(filt, cons, duals, filt_out, cons_out, duals_out, stacked):
    stacked[:, 6 * LANES :] = jnp.zeros((6 * M, LANES), BF16)
    for i, ref in enumerate((filt, cons, duals)):
        for j, part in enumerate(split2(ref[...])):
            at = (2 * i + j) * M
            stacked[at : at + M, :FLAT] = part
    source = lax.broadcasted_iota(jnp.int32, (WIDE, LANES), 0)
    lane = lane_of(WIDE)
    for a in range(K):
        pick = (source == flat_of(lane + a * LANES)).astype(F32).astype(BF16)
        moved = matmul(stacked[...], pick)
        for i, ref in enumerate((filt_out, cons_out, duals_out)):
            at = 2 * i * M
            ref[a * M : (a + 1) * M, :] = moved[at : at + M] + moved[at + M : at + 2 * M]


def padded_row(y, size, own, above, below):
    if y < REACH:
        return above[y * size : (y + 1) * size, :]
    if y < REACH + ROWS:
        at = (y - REACH) * size
        return own[at : at + size, :]
    at = (y - REACH - ROWS) * size
    return below[at : at + size, :]


def pack_kernel(size, own, above, below, left_edge, right_edge):
    lane = lane_of(size)
    left = jnp.zeros((size, LANES), F32)
    right = jnp.zeros((size, LANES), F32)
    for y in range(PAD_ROWS):
        value = padded_row(y, size, own, above, below)
        here = (lane >= 3 * y) & (lane < 3 * y + 3)
        left = jnp.where(here, roll(value, 3 * y), left)
        right = jnp.where(here, roll(value, 3 * y + 3), right)
    left_edge[...] = left
    right_edge[...] = right


def neighbours(axis, toward_high, toward_low):
    count = lax.axis_size(axis)
    odd = lax.axis_index(axis) % 2 == 1
    even_pairs = [(i, i ^ 1) for i in range(count)]
    odd_pairs = [(i, i + 1 if i % 2 == 1 else i - 1) for i in range(1, count - 1)]
    first = lax.ppermute(jnp.where(odd, toward_low, toward_high), axis, even_pairs)
    second = lax.ppermute(jnp.where(odd, toward_high, toward_low), axis, odd_pairs)
    return jnp.where(odd, first, second), jnp.where(odd, second, first)


def pack(size, own, above, below):
    return call(functools.partial(pack_kernel, size), [shape(size, LANES)] * 2)(own, above, below)


def halos(size, own, top, bottom):
    above, below = neighbours("row", bottom, top)
    left_edge, right_edge = pack(size, own, above, below)
    left, right = neighbours("col", right_edge, left_edge)
    return above, below, left, right


def recon_and_grad(
    maps, above, below, left, right, observed, filt,
    resid_out, top, bottom, grad, x_hi, x_lo, h_hi, h_lo, r_all, r_edge,
):
    for y in range(PAD_ROWS):
        hi, lo = split2(padded_row(y, M, maps, above, below))
        for ref, part in ((x_hi, hi), (x_lo, lo)):
            ref[y * M : (y + 1) * M, :LANES] = part
            if y > 0:
                ref[(y - 1) * M : y * M, LANES:] = part
    for ref in (x_hi, x_lo):
        ref[(PAD_ROWS - 1) * M :, LANES:] = jnp.zeros((M, LANES), BF16)
    edge = jnp.where(lane_of(M) < 64, right[...], roll(left[...], 64))
    for a in range(K):
        hi, lo = split2(roll(edge, -3 * a))
        h_hi[a * M : (a + 1) * M, :] = hi
        h_lo[a * M : (a + 1) * M, :] = lo
    for ref in (h_hi, h_lo):
        ref[D_ROWS:, :] = jnp.zeros((SLAB - D_ROWS, LANES), BF16)

    turned = jnp.concatenate([filt, jnp.zeros((SLAB - D_ROWS, LANES), F32)], axis=0).T
    d_hi, d_lo = split2(turned)
    d_both = jnp.concatenate([d_hi, d_lo], axis=0)

    def apply(hi, lo):
        both = matmul(d_both, hi)
        return both[:LANES] + both[LANES:] + matmul(d_hi, lo)

    lane = lane_of(C)
    at_edge = apply(h_hi[...], h_lo[...])
    resid = []
    for y in range(0, ROWS, 2):
        planes = apply(x_hi[y * M : y * M + SLAB, :], x_lo[y * M : y * M + SLAB, :])
        for k in range(2):
            row = y + k
            total = jnp.zeros((C, LANES), F32)
            for b in range(K):
                d = b - REACH
                own = roll(planes[b * C : (b + 1) * C, k * LANES : (k + 1) * LANES], -d)
                band_edge = at_edge[b * C : (b + 1) * C, :]
                if d > 0:
                    moved = roll(band_edge, 131 - b - 3 * row)
                    own = jnp.where(lane >= LANES - d, moved, own)
                elif d < 0:
                    moved = roll(band_edge, -(64 + 3 * row) - b)
                    own = jnp.where(lane < -d, moved, own)
                total = total + own
            value = norm_scale * total - observed[:, row, :]
            resid.append(value)
            resid_out[row * C : (row + 1) * C, :] = value
            if row < REACH:
                top[row * C : (row + 1) * C, :] = value
            if row >= ROWS - REACH:
                at = (row - ROWS + REACH) * C
                bottom[at : at + C, :] = value

    zero16 = jnp.zeros((C, LANES), F32)
    for b in range(K):
        d = b - REACH
        near = zero16
        for row in range(ROWS):
            moved = roll(resid[row], d)
            if d > 0:
                moved = jnp.where(lane >= d, moved, 0.0)
                here = (lane >= 3 * row) & (lane < 3 * row + d)
                near = jnp.where(here, roll(resid[row], 3 * row - 131 + b), near)
            elif d < 0:
                moved = jnp.where(lane < LANES + d, moved, 0.0)
                here = (lane >= 64 + 3 * row + b) & (lane < 64 + 3 * row + 3)
                near = jnp.where(here, roll(resid[row], 64 + 3 * row + b), near)
            hi, lo = split2(moved)
            r_all[b * C : (b + 1) * C, row * LANES : (row + 1) * LANES] = hi
            r_all[LANES + b * C : LANES + (b + 1) * C, row * LANES : (row + 1) * LANES] = lo
        hi, lo = split2(near)
        r_edge[b * C : (b + 1) * C, :] = hi
        r_edge[LANES + b * C : LANES + (b + 1) * C, :] = lo
    for at in (K * C, LANES + K * C):
        r_all[at : at + C, :] = jnp.zeros((C, ROWS * LANES), BF16)
        r_edge[at : at + C, :] = jnp.zeros((C, LANES), BF16)

    def gather(hi, lo, spread):
        both = matmul_nt(hi, spread)
        return both[:, :LANES] + both[:, LANES:] + matmul_nt(lo, spread[:LANES])

    total = gather(h_hi[:D_ROWS, :], h_lo[:D_ROWS, :], r_edge[...])
    for y in range(0, ROWS, 2):
        total = total + gather(
            x_hi[y * M : y * M + D_ROWS, :],
            x_lo[y * M : y * M + D_ROWS, :],
            r_all[:, y * LANES : (y + 2) * LANES],
        )
    grad[...] = total


RECON_OUT = [shape(ROWS * C, LANES), shape(3 * C, LANES), shape(3 * C, LANES), shape(G_ROWS, LANES)]
RECON_SCRATCH = [
    pltpu.VMEM((PAD_ROWS * M, 2 * LANES), BF16),
    pltpu.VMEM((PAD_ROWS * M, 2 * LANES), BF16),
    pltpu.VMEM((SLAB, LANES), BF16),
    pltpu.VMEM((SLAB, LANES), BF16),
    pltpu.VMEM((2 * LANES, ROWS * LANES), BF16),
    pltpu.VMEM((2 * LANES, LANES), BF16),
]


def updated(summed, filt, cons, duals, keep):
    squares = jnp.zeros((M, LANES), F32)
    for a in range(K):
        at = slice(a * M, (a + 1) * M)
        now, dual = filt[at, :], duals[at, :]
        after = now - dict_step * (norm_scale * summed[at, :] + penalty * (now - cons[at, :] + dual))
        joined = after + dual
        squares = squares + joined * joined
        keep(0, a, after)
        keep(1, a, joined)
    spread = jnp.sqrt(jnp.sum(squares, axis=1, keepdims=True) / FLAT)
    return 1.0 / jnp.maximum(1.0, spread)


def first_kernel(maps, above, below, left, right, observed, filt, *rest):
    recon_and_grad(maps, above, below, left, right, observed, filt[...], *rest)


def next_kernel(
    summed, filt, cons, duals, maps, above, below, left, right, observed,
    filt_out, cons_out, duals_out, *rest,
):
    update_into(summed, filt, cons, duals, filt_out, cons_out, duals_out)
    recon_and_grad(maps, above, below, left, right, observed, filt_out[...], *rest)


def update_into(summed, filt, cons, duals, filt_out, cons_out, duals_out):
    refs = (filt_out, cons_out)

    def keep(which, a, value):
        refs[which][a * M : (a + 1) * M, :] = value

    factor = updated(summed, filt, cons, duals, keep)
    for a in range(K):
        at = slice(a * M, (a + 1) * M)
        joined = cons_out[at, :]
        projected = joined * factor
        cons_out[at, :] = projected
        duals_out[at, :] = joined - projected


def last_kernel(summed, filt, cons, duals, filt_out, cons_out, duals_out, new, stacked):
    update_into(summed, filt, cons, duals, new.at[0], new.at[1], new.at[2])
    for i in range(3):
        for a in range(K):
            for j, part in enumerate(split2(new[i, a * M : (a + 1) * M, :])):
                at = (2 * i + j) * M
                stacked[at : at + M, a * LANES : (a + 1) * LANES] = part
    source = lax.broadcasted_iota(jnp.int32, (WIDE, LANES), 0)
    wanted = flat_of(source)
    for block in range(K):
        target = lane_of(WIDE) + block * LANES
        pick = (wanted == target).astype(F32).astype(BF16)
        moved = matmul(stacked[...], pick)
        width = min(LANES, FLAT - block * LANES)
        for i, ref in enumerate((filt_out, cons_out, duals_out)):
            at = 2 * i * M
            value = moved[at : at + M] + moved[at + M : at + 2 * M]
            ref[:, block * LANES : block * LANES + width] = value[:, :width]


def corr_kernel(last, resid, above, below, left, right, filt, maps, *rest):
    if last:
        maps_out, s_hi, s_lo = rest
    else:
        maps_out, top, bottom, s_hi, s_lo = rest
    lane = lane_of(C)
    for y in range(PAD_ROWS - 1 + 1):
        own = padded_row(y, C, resid, above, below)
        edge = jnp.where(lane < 3, roll(right[...], -3 * y), roll(left[...], 125 - 3 * y))
        for b in range(K + 1):
            if b < K:
                d = b - REACH
                value = own
                if d > 0:
                    value = jnp.where(lane >= LANES - d, edge, own)
                elif d < 0:
                    value = jnp.where(lane < -d, edge, own)
                hi, lo = split2(roll(value, d))
            else:
                hi = lo = jnp.zeros((C, LANES), BF16)
            for ref, part in ((s_hi, hi), (s_lo, lo)):
                at = y * LANES + b * C
                if y < PAD_ROWS - 1:
                    ref[at : at + C, :LANES] = part
                if y > 0:
                    ref[at - LANES : at - LANES + C, LANES:] = part

    across = jnp.concatenate([filt[(6 - q) * M : (7 - q) * M, :] for q in range(K)], axis=1)
    d_hi, d_lo = split2(across)
    d_both = jnp.concatenate([d_hi, d_lo], axis=0)
    limit = step_coef * sparsity
    for y in range(0, ROWS, 2):
        slab = slice(y * LANES, y * LANES + WIDE)
        both = matmul(d_both, s_hi[slab, :])
        corr = both[:M] + both[M:] + matmul(d_hi, s_lo[slab, :])
        for k in range(2):
            row = y + k
            moved = maps[row * M : (row + 1) * M, :] - (step_coef * norm_scale) * corr[
                :, k * LANES : (k + 1) * LANES
            ]
            value = moved - jnp.clip(moved, -limit, limit)
            if last:
                maps_out[:, row, :] = value
                continue
            maps_out[row * M : (row + 1) * M, :] = value
            if row < REACH:
                top[row * M : (row + 1) * M, :] = value
            if row >= ROWS - REACH:
                at = (row - ROWS + REACH) * M
                bottom[at : at + M, :] = value


CORR_SCRATCH = [pltpu.VMEM(((PAD_ROWS - 1) * LANES, 2 * LANES), BF16)] * 2


def swap_even(i):
    return i ^ 1


def swap_odd(i, count):
    return (i + 1) % count if i % 2 == 1 else (i - 1) % count


THIRD = {2: 5, 5: 2, 1: 6, 6: 1, 3: 0, 0: 3, 4: 7, 7: 4}
CORE = [(i, i ^ 1) for i in range(8)]
Y_EVEN = [(2 * y + core, 2 * swap_even(y) + core) for y in range(4) for core in range(2)]
Y_ODD = [(2 * y + core, 2 * swap_odd(y, 4) + core) for y in range(4) for core in range(2)]


def pairs_col(change):
    return [(8 * x + z, change(x, z)) for x in range(4) for z in range(8)]


COLS = [
    pairs_col(lambda x, z: swap_even(x) * 8 + z),
    pairs_col(lambda x, z: swap_odd(x, 4) * 8 + z),
    pairs_col(lambda x, z: x * 8 + swap_even(z)),
    pairs_col(lambda x, z: x * 8 + swap_odd(z, 8)),
    pairs_col(lambda x, z: x * 8 + THIRD[z]),
]


def halves(value, bit):
    half = value.shape[0] // 2
    low, high = value[:half], value[half:]
    return jnp.where(bit, low, high), jnp.where(bit, high, low)


def joined(mine, other, bit):
    return jnp.where(bit, jnp.concatenate([other, mine]), jnp.concatenate([mine, other]))


def sum_all(grad, state, side):
    row = lax.axis_index("row")
    y = row // 2
    upper = (y == 1) | (y == 2)
    odd_core = row % 2 == 1
    value = grad

    def beside(k, sent, axis, pairs, kept):
        nonlocal state
        sent, kept, state = lax.optimization_barrier((sent, kept, state))
        other = lax.ppermute(sent, axis, pairs)
        if k in side:
            state = side[k](state)
        return kept, other

    for k, bit, pairs in ((0, odd_core, CORE), (1, upper, Y_EVEN)):
        sent, kept = halves(value, bit)
        kept, other = beside(k, sent, "row", pairs, kept)
        value = kept + other
    steps = [("row", Y_ODD)] + [("col", pairs) for pairs in COLS]
    for k, (axis, pairs) in enumerate(steps):
        kept, other = beside(2 + k, value, axis, pairs, value)
        value = kept + other
    for k, bit, pairs in ((8, upper, Y_EVEN), (9, odd_core, CORE)):
        kept, other = beside(k, value, "row", pairs, value)
        value = joined(kept, other, bit)
    return value, state


def local(observed, coef_maps, dictionary, consensus, dual_vars):
    map_rows = [shape(ROWS * M, LANES), shape(3 * M, LANES), shape(3 * M, LANES)]
    filters = [shape(D_ROWS, LANES)] * 3
    maps, top, bottom = call(rows_kernel, map_rows)(coef_maps)
    filt, cons, duals = call(to_rows_kernel, filters, [pltpu.VMEM((6 * M, WIDE), BF16)])(
        dictionary, consensus, dual_vars
    )
    edges = halos(M, maps, top, bottom)
    resid, r_top, r_bottom, grad = call(first_kernel, RECON_OUT, RECON_SCRATCH)(
        maps, *edges, observed, filt
    )

    def resid_rows(state):
        resid, top, bottom, filt, maps = state
        return resid, neighbours("row", bottom, top), filt, maps

    def resid_columns(state):
        resid, around, filt, maps = state
        left_edge, right_edge = pack(C, resid, *around)
        return resid, (*around, *neighbours("col", right_edge, left_edge)), filt, maps

    def threshold(last, outs):
        def run(state):
            resid, around, filt, maps = state
            return call(functools.partial(corr_kernel, last), outs, CORR_SCRATCH)(
                resid, *around, filt, maps
            )

        return run

    def map_rows_out(state):
        maps, top, bottom = state
        return maps, neighbours("row", bottom, top)

    def map_pack(state):
        maps, around = state
        return maps, around, pack(M, maps, *around)

    def map_columns(state):
        maps, around, (left_edge, right_edge) = state
        return maps, (*around, *neighbours("col", right_edge, left_edge))

    summed, (maps, edges) = sum_all(
        grad,
        (resid, r_top, r_bottom, filt, maps),
        {
            0: resid_rows,
            1: resid_columns,
            2: threshold(False, map_rows),
            3: map_rows_out,
            5: map_pack,
            7: map_columns,
        },
    )
    filt, cons, duals, resid, r_top, r_bottom, grad = call(
        next_kernel, filters + RECON_OUT, RECON_SCRATCH
    )(summed, filt, cons, duals, maps, *edges, observed)
    summed, new_maps = sum_all(
        grad,
        (resid, r_top, r_bottom, filt, maps),
        {2: resid_rows, 7: resid_columns, 8: threshold(True, shape(M, ROWS, LANES))},
    )
    new = call(
        last_kernel,
        [shape(M, FLAT)] * 3,
        [pltpu.VMEM((3, D_ROWS, LANES), F32), pltpu.VMEM((6 * M, WIDE), BF16)],
    )(summed, filt, cons, duals)
    return (new_maps, *new)


def solution(mesh):
    return jax.shard_map(
        local,
        mesh=mesh,
        in_specs=(P(None, "row", "col"), P(None, "row", "col"), P(), P(), P()),
        out_specs=(P(None, "row", "col"), P(), P(), P()),
        check_vma=False,
    )
```

```python
import functools
import math

import jax
import jax.numpy as jnp
from jax import lax
from jax.experimental import pallas as pl
from jax.experimental.pallas import tpu as pltpu
from jax.sharding import PartitionSpec as P

M = 96
C = 16
K = 7
REACH = 3
ITERS = 2
ROWS = 8
LANES = 128
PAD_ROWS = ROWS + 2 * REACH
TAPS = K * K
FLAT = C * TAPS
WIDE = K * LANES
D_ROWS = K * M
G_ROWS = D_ROWS
SLAB = 8 * M

step_coef = 0.5
sparsity = 0.1
dict_step = 0.08
penalty = 2.0
norm_scale = 1.0 / math.sqrt(M * K * K)

F32 = jnp.float32
BF16 = jnp.bfloat16


def shape(*dims):
    return jax.ShapeDtypeStruct(dims, F32)


def call(kernel, outs, scratch=()):
    return pl.pallas_call(
        kernel,
        out_shape=outs,
        scratch_shapes=list(scratch),
        compiler_params=pltpu.CompilerParams(vmem_limit_bytes=28 * 1024 * 1024),
    )


def split2(value):
    high = value.astype(BF16)
    return high, (value - high.astype(F32)).astype(BF16)


def roll(value, shift):
    shift = shift % LANES
    return value if shift == 0 else pltpu.roll(value, shift, 1)


def lane_of(rows):
    return lax.broadcasted_iota(jnp.int32, (rows, LANES), 1)


def matmul(a, b):
    return jnp.dot(a, b, preferred_element_type=F32)


def matmul_nt(a, b):
    return lax.dot_general(a, b, (((1,), (1,)), ((), ())), preferred_element_type=F32)


def rows_kernel(maps, by_row, top, bottom):
    for y in range(ROWS):
        value = maps[:, y, :]
        by_row[y * M : (y + 1) * M, :] = value
        if y < REACH:
            top[y * M : (y + 1) * M, :] = value
        if y >= ROWS - REACH:
            at = (y - ROWS + REACH) * M
            bottom[at : at + M, :] = value


def flat_of(lane):
    row_tap = lane >> 7
    col_tap = (lane >> 4) & 7
    band = lane & 15
    return jnp.where(col_tap < K, band * TAPS + row_tap * K + col_tap, -1)


def to_rows_kernel(filt, cons, duals, filt_out, cons_out, duals_out, stacked):
    stacked[:, 6 * LANES :] = jnp.zeros((6 * M, LANES), BF16)
    for i, ref in enumerate((filt, cons, duals)):
        for j, part in enumerate(split2(ref[...])):
            at = (2 * i + j) * M
            stacked[at : at + M, :FLAT] = part
    source = lax.broadcasted_iota(jnp.int32, (WIDE, LANES), 0)
    lane = lane_of(WIDE)
    for a in range(K):
        pick = (source == flat_of(lane + a * LANES)).astype(F32).astype(BF16)
        moved = matmul(stacked[...], pick)
        for i, ref in enumerate((filt_out, cons_out, duals_out)):
            at = 2 * i * M
            ref[a * M : (a + 1) * M, :] = moved[at : at + M] + moved[at + M : at + 2 * M]


def padded_row(y, size, own, above, below):
    if y < REACH:
        return above[y * size : (y + 1) * size, :]
    if y < REACH + ROWS:
        at = (y - REACH) * size
        return own[at : at + size, :]
    at = (y - REACH - ROWS) * size
    return below[at : at + size, :]


def pack_kernel(size, own, above, below, left_edge, right_edge):
    lane = lane_of(size)
    left = jnp.zeros((size, LANES), F32)
    right = jnp.zeros((size, LANES), F32)
    for y in range(PAD_ROWS):
        value = padded_row(y, size, own, above, below)
        here = (lane >= 3 * y) & (lane < 3 * y + 3)
        left = jnp.where(here, roll(value, 3 * y), left)
        right = jnp.where(here, roll(value, 3 * y + 3), right)
    left_edge[...] = left
    right_edge[...] = right


def neighbours(axis, toward_high, toward_low):
    count = lax.axis_size(axis)
    odd = lax.axis_index(axis) % 2 == 1
    even_pairs = [(i, i ^ 1) for i in range(count)]
    odd_pairs = [(i, i + 1 if i % 2 == 1 else i - 1) for i in range(1, count - 1)]
    first = lax.ppermute(jnp.where(odd, toward_low, toward_high), axis, even_pairs)
    second = lax.ppermute(jnp.where(odd, toward_high, toward_low), axis, odd_pairs)
    return jnp.where(odd, first, second), jnp.where(odd, second, first)


def pack(size, own, above, below):
    return call(functools.partial(pack_kernel, size), [shape(size, LANES)] * 2)(own, above, below)


def halos(size, own, top, bottom):
    above, below = neighbours("row", bottom, top)
    left_edge, right_edge = pack(size, own, above, below)
    left, right = neighbours("col", right_edge, left_edge)
    return above, below, left, right


def recon_and_grad(
    maps, above, below, left, right, observed, filt,
    resid_out, top, bottom, grad, x_hi, x_lo, h_hi, h_lo, r_all, r_edge,
):
    for y in range(PAD_ROWS):
        hi, lo = split2(padded_row(y, M, maps, above, below))
        for ref, part in ((x_hi, hi), (x_lo, lo)):
            ref[y * M : (y + 1) * M, :LANES] = part
            if y > 0:
                ref[(y - 1) * M : y * M, LANES:] = part
    for ref in (x_hi, x_lo):
        ref[(PAD_ROWS - 1) * M :, LANES:] = jnp.zeros((M, LANES), BF16)
    edge = jnp.where(lane_of(M) < 64, right[...], roll(left[...], 64))
    for a in range(K):
        hi, lo = split2(roll(edge, -3 * a))
        h_hi[a * M : (a + 1) * M, :] = hi
        h_lo[a * M : (a + 1) * M, :] = lo
    for ref in (h_hi, h_lo):
        ref[D_ROWS:, :] = jnp.zeros((SLAB - D_ROWS, LANES), BF16)

    turned = jnp.concatenate([filt, jnp.zeros((SLAB - D_ROWS, LANES), F32)], axis=0).T
    d_hi, d_lo = split2(turned)
    d_both = jnp.concatenate([d_hi, d_lo], axis=0)

    def apply(hi, lo):
        both = matmul(d_both, hi)
        return both[:LANES] + both[LANES:] + matmul(d_hi, lo)

    lane = lane_of(C)
    at_edge = apply(h_hi[...], h_lo[...])
    resid = []
    for y in range(0, ROWS, 2):
        planes = apply(x_hi[y * M : y * M + SLAB, :], x_lo[y * M : y * M + SLAB, :])
        for k in range(2):
            row = y + k
            total = jnp.zeros((C, LANES), F32)
            for b in range(K):
                d = b - REACH
                own = roll(planes[b * C : (b + 1) * C, k * LANES : (k + 1) * LANES], -d)
                band_edge = at_edge[b * C : (b + 1) * C, :]
                if d > 0:
                    moved = roll(band_edge, 131 - b - 3 * row)
                    own = jnp.where(lane >= LANES - d, moved, own)
                elif d < 0:
                    moved = roll(band_edge, -(64 + 3 * row) - b)
                    own = jnp.where(lane < -d, moved, own)
                total = total + own
            value = norm_scale * total - observed[:, row, :]
            resid.append(value)
            resid_out[row * C : (row + 1) * C, :] = value
            if row < REACH:
                top[row * C : (row + 1) * C, :] = value
            if row >= ROWS - REACH:
                at = (row - ROWS + REACH) * C
                bottom[at : at + C, :] = value

    zero16 = jnp.zeros((C, LANES), F32)
    for b in range(K):
        d = b - REACH
        near = zero16
        for row in range(ROWS):
            moved = roll(resid[row], d)
            if d > 0:
                moved = jnp.where(lane >= d, moved, 0.0)
                here = (lane >= 3 * row) & (lane < 3 * row + d)
                near = jnp.where(here, roll(resid[row], 3 * row - 131 + b), near)
            elif d < 0:
                moved = jnp.where(lane < LANES + d, moved, 0.0)
                here = (lane >= 64 + 3 * row + b) & (lane < 64 + 3 * row + 3)
                near = jnp.where(here, roll(resid[row], 64 + 3 * row + b), near)
            hi, lo = split2(moved)
            r_all[b * C : (b + 1) * C, row * LANES : (row + 1) * LANES] = hi
            r_all[LANES + b * C : LANES + (b + 1) * C, row * LANES : (row + 1) * LANES] = lo
        hi, lo = split2(near)
        r_edge[b * C : (b + 1) * C, :] = hi
        r_edge[LANES + b * C : LANES + (b + 1) * C, :] = lo
    for at in (K * C, LANES + K * C):
        r_all[at : at + C, :] = jnp.zeros((C, ROWS * LANES), BF16)
        r_edge[at : at + C, :] = jnp.zeros((C, LANES), BF16)

    def gather(hi, lo, spread):
        both = matmul_nt(hi, spread)
        return both[:, :LANES] + both[:, LANES:] + matmul_nt(lo, spread[:LANES])

    total = gather(h_hi[:D_ROWS, :], h_lo[:D_ROWS, :], r_edge[...])
    for y in range(0, ROWS, 2):
        total = total + gather(
            x_hi[y * M : y * M + D_ROWS, :],
            x_lo[y * M : y * M + D_ROWS, :],
            r_all[:, y * LANES : (y + 2) * LANES],
        )
    grad[...] = total


RECON_OUT = [shape(ROWS * C, LANES), shape(3 * C, LANES), shape(3 * C, LANES), shape(G_ROWS, LANES)]
RECON_SCRATCH = [
    pltpu.VMEM((PAD_ROWS * M, 2 * LANES), BF16),
    pltpu.VMEM((PAD_ROWS * M, 2 * LANES), BF16),
    pltpu.VMEM((SLAB, LANES), BF16),
    pltpu.VMEM((SLAB, LANES), BF16),
    pltpu.VMEM((2 * LANES, ROWS * LANES), BF16),
    pltpu.VMEM((2 * LANES, LANES), BF16),
]


def updated(summed, filt, cons, duals, keep):
    squares = jnp.zeros((M, LANES), F32)
    for a in range(K):
        at = slice(a * M, (a + 1) * M)
        now, dual = filt[at, :], duals[at, :]
        after = now - dict_step * (norm_scale * summed[at, :] + penalty * (now - cons[at, :] + dual))
        joined = after + dual
        squares = squares + joined * joined
        keep(0, a, after)
        keep(1, a, joined)
    spread = jnp.sqrt(jnp.sum(squares, axis=1, keepdims=True) / FLAT)
    return 1.0 / jnp.maximum(1.0, spread)


def first_kernel(maps, above, below, left, right, observed, filt, *rest):
    recon_and_grad(maps, above, below, left, right, observed, filt[...], *rest)


def next_kernel(
    summed, filt, cons, duals, maps, above, below, left, right, observed,
    filt_out, cons_out, duals_out, *rest,
):
    update_into(summed, filt, cons, duals, filt_out, cons_out, duals_out)
    recon_and_grad(maps, above, below, left, right, observed, filt_out[...], *rest)


def update_into(summed, filt, cons, duals, filt_out, cons_out, duals_out):
    refs = (filt_out, cons_out)

    def keep(which, a, value):
        refs[which][a * M : (a + 1) * M, :] = value

    factor = updated(summed, filt, cons, duals, keep)
    for a in range(K):
        at = slice(a * M, (a + 1) * M)
        joined = cons_out[at, :]
        projected = joined * factor
        cons_out[at, :] = projected
        duals_out[at, :] = joined - projected


def last_kernel(summed, filt, cons, duals, filt_out, cons_out, duals_out, new, stacked):
    update_into(summed, filt, cons, duals, new.at[0], new.at[1], new.at[2])
    for i in range(3):
        for a in range(K):
            for j, part in enumerate(split2(new[i, a * M : (a + 1) * M, :])):
                at = (2 * i + j) * M
                stacked[at : at + M, a * LANES : (a + 1) * LANES] = part
    source = lax.broadcasted_iota(jnp.int32, (WIDE, LANES), 0)
    wanted = flat_of(source)
    for block in range(K):
        target = lane_of(WIDE) + block * LANES
        pick = (wanted == target).astype(F32).astype(BF16)
        moved = matmul(stacked[...], pick)
        width = min(LANES, FLAT - block * LANES)
        for i, ref in enumerate((filt_out, cons_out, duals_out)):
            at = 2 * i * M
            value = moved[at : at + M] + moved[at + M : at + 2 * M]
            ref[:, block * LANES : block * LANES + width] = value[:, :width]


def corr_kernel(last, resid, above, below, left, right, filt, maps, *rest):
    if last:
        maps_out, s_hi, s_lo = rest
    else:
        maps_out, top, bottom, s_hi, s_lo = rest
    lane = lane_of(C)
    for y in range(PAD_ROWS - 1 + 1):
        own = padded_row(y, C, resid, above, below)
        edge = jnp.where(lane < 3, roll(right[...], -3 * y), roll(left[...], 125 - 3 * y))
        for b in range(K + 1):
            if b < K:
                d = b - REACH
                value = own
                if d > 0:
                    value = jnp.where(lane >= LANES - d, edge, own)
                elif d < 0:
                    value = jnp.where(lane < -d, edge, own)
                hi, lo = split2(roll(value, d))
            else:
                hi = lo = jnp.zeros((C, LANES), BF16)
            for ref, part in ((s_hi, hi), (s_lo, lo)):
                at = y * LANES + b * C
                if y < PAD_ROWS - 1:
                    ref[at : at + C, :LANES] = part
                if y > 0:
                    ref[at - LANES : at - LANES + C, LANES:] = part

    across = jnp.concatenate([filt[(6 - q) * M : (7 - q) * M, :] for q in range(K)], axis=1)
    d_hi, d_lo = split2(across)
    d_both = jnp.concatenate([d_hi, d_lo], axis=0)
    limit = step_coef * sparsity
    for y in range(0, ROWS, 2):
        slab = slice(y * LANES, y * LANES + WIDE)
        both = matmul(d_both, s_hi[slab, :])
        corr = both[:M] + both[M:] + matmul(d_hi, s_lo[slab, :])
        for k in range(2):
            row = y + k
            moved = maps[row * M : (row + 1) * M, :] - (step_coef * norm_scale) * corr[
                :, k * LANES : (k + 1) * LANES
            ]
            value = moved - jnp.clip(moved, -limit, limit)
            if last:
                maps_out[:, row, :] = value
                continue
            maps_out[row * M : (row + 1) * M, :] = value
            if row < REACH:
                top[row * M : (row + 1) * M, :] = value
            if row >= ROWS - REACH:
                at = (row - ROWS + REACH) * M
                bottom[at : at + M, :] = value


CORR_SCRATCH = [pltpu.VMEM(((PAD_ROWS - 1) * LANES, 2 * LANES), BF16)] * 2


def swap_even(i):
    return i ^ 1


def swap_odd(i, count):
    return (i + 1) % count if i % 2 == 1 else (i - 1) % count


THIRD = {2: 5, 5: 2, 1: 6, 6: 1, 3: 0, 0: 3, 4: 7, 7: 4}
CORE = [(i, i ^ 1) for i in range(8)]
Y_EVEN = [(2 * y + core, 2 * swap_even(y) + core) for y in range(4) for core in range(2)]
Y_ODD = [(2 * y + core, 2 * swap_odd(y, 4) + core) for y in range(4) for core in range(2)]


def pairs_col(change):
    return [(8 * x + z, change(x, z)) for x in range(4) for z in range(8)]


COLS = [
    pairs_col(lambda x, z: swap_even(x) * 8 + z),
    pairs_col(lambda x, z: swap_odd(x, 4) * 8 + z),
    pairs_col(lambda x, z: x * 8 + swap_even(z)),
    pairs_col(lambda x, z: x * 8 + swap_odd(z, 8)),
    pairs_col(lambda x, z: x * 8 + THIRD[z]),
]


def halves(value, bit):
    half = value.shape[0] // 2
    low, high = value[:half], value[half:]
    return jnp.where(bit, low, high), jnp.where(bit, high, low)


def joined(mine, other, bit):
    return jnp.where(bit, jnp.concatenate([other, mine]), jnp.concatenate([mine, other]))


def sum_all(grad, state, side):
    row = lax.axis_index("row")
    y = row // 2
    upper = (y == 1) | (y == 2)
    odd_core = row % 2 == 1
    value = grad

    def beside(k, sent, axis, pairs, kept):
        nonlocal state
        sent, kept, state = lax.optimization_barrier((sent, kept, state))
        other = lax.ppermute(sent, axis, pairs)
        if k in side:
            state = side[k](state)
        return kept, other

    for k, bit, pairs in ((0, odd_core, CORE), (1, upper, Y_EVEN)):
        sent, kept = halves(value, bit)
        kept, other = beside(k, sent, "row", pairs, kept)
        value = kept + other
    steps = [("row", Y_ODD)] + [("col", pairs) for pairs in COLS]
    for k, (axis, pairs) in enumerate(steps):
        kept, other = beside(2 + k, value, axis, pairs, value)
        value = kept + other
    for k, bit, pairs in ((8, upper, Y_EVEN), (9, odd_core, CORE)):
        kept, other = beside(k, value, "row", pairs, value)
        value = joined(kept, other, bit)
    return value, state


def local(observed, coef_maps, dictionary, consensus, dual_vars):
    map_rows = [shape(ROWS * M, LANES), shape(3 * M, LANES), shape(3 * M, LANES)]
    filters = [shape(D_ROWS, LANES)] * 3
    maps, top, bottom = call(rows_kernel, map_rows)(coef_maps)
    filt, cons, duals = call(to_rows_kernel, filters, [pltpu.VMEM((6 * M, WIDE), BF16)])(
        dictionary, consensus, dual_vars
    )
    edges = halos(M, maps, top, bottom)
    resid, r_top, r_bottom, grad = call(first_kernel, RECON_OUT, RECON_SCRATCH)(
        maps, *edges, observed, filt
    )

    def resid_rows(state):
        resid, top, bottom, filt, maps = state
        return resid, neighbours("row", bottom, top), filt, maps

    def resid_columns(state):
        resid, around, filt, maps = state
        left_edge, right_edge = pack(C, resid, *around)
        return resid, (*around, *neighbours("col", right_edge, left_edge)), filt, maps

    def threshold(last, outs):
        def run(state):
            resid, around, filt, maps = state
            return call(functools.partial(corr_kernel, last), outs, CORR_SCRATCH)(
                resid, *around, filt, maps
            )

        return run

    def map_rows_out(state):
        maps, top, bottom = state
        return maps, neighbours("row", bottom, top)

    def map_pack(state):
        maps, around = state
        return maps, around, pack(M, maps, *around)

    def map_columns(state):
        maps, around, (left_edge, right_edge) = state
        return maps, (*around, *neighbours("col", right_edge, left_edge))

    summed, (maps, edges) = sum_all(
        grad,
        (resid, r_top, r_bottom, filt, maps),
        {
            0: resid_rows,
            1: resid_columns,
            2: threshold(False, map_rows),
            3: map_rows_out,
            5: map_pack,
            7: map_columns,
        },
    )
    filt, cons, duals, resid, r_top, r_bottom, grad = call(
        next_kernel, filters + RECON_OUT, RECON_SCRATCH
    )(summed, filt, cons, duals, maps, *edges, observed)
    summed, new_maps = sum_all(
        grad,
        (resid, r_top, r_bottom, filt, maps),
        {0: resid_rows, 1: resid_columns, 2: threshold(True, shape(M, ROWS, LANES))},
    )
    new = call(
        last_kernel,
        [shape(M, FLAT)] * 3,
        [pltpu.VMEM((3, D_ROWS, LANES), F32), pltpu.VMEM((6 * M, WIDE), BF16)],
    )(summed, filt, cons, duals)
    return (new_maps, *new)


def solution(mesh):
    return jax.shard_map(
        local,
        mesh=mesh,
        in_specs=(P(None, "row", "col"), P(None, "row", "col"), P(), P(), P()),
        out_specs=(P(None, "row", "col"), P(), P(), P()),
        check_vma=False,
    )
```
